32 devices in a mesh: row: 8 (over z, x), col: 4 (over y, core).
Axes of the slice: x: 2, y: 2, z: 4, core: 2. Of those that a mesh axis runs over, the one named last changes fastest.
Arguments:
- estimate: float32 [8, 256, 512], P(None, 'row', 'col'), may hold values from 0.5 to 2
- views_data: bfloat16 [4, 8, 256, 512], P(None, None, 'row', 'col'), may hold values from 0.25 to 4
- psf_rows: float32 [4, 33], replicated, may hold values from 0.05 to 1
- psf_cols: float32 [4, 33], replicated, may hold values from 0.05 to 1
Outputs:
- estimate_next: float32 [8, 256, 512], P(None, 'row', 'col')
The draws below stay inside these ranges and needn't reach their ends.
All inputs are finite; a program needn't handle non-finite values.
Results may differ from the reference program's by a relative error of at most 0.0003.
Values may be sent and summed in bfloat16 or wider, within the bound.
A program may use at most 64 MiB of HBM per device.

```python
import math
import jax
import jax.numpy as jnp
from jax import lax

VIEWS = 4
KW = 33
PLANES = 8
NY = 256
NX = 512


def level_of(stream_key, shape, split, least, high):
    level, own = 1.0, jax.random.fold_in(stream_key, 6)
    for position, parts in split:
        draws = jnp.exp(jax.random.uniform(jax.random.fold_in(own, position), (parts,), jnp.float32, least / len(split), high / len(split)))
        level = level * jnp.repeat(draws, shape[position] // parts).reshape([-1 if axis == position else 1 for axis in range(len(shape))])
    return level


def setup_inputs(seed: int = 0) -> dict:
    arg_keys = jax.random.split(jax.random.key(seed), 5)
    estimate = jnp.clip(0.5 + 1.5 * jax.random.uniform(arg_keys[0], (PLANES, NY, NX), jnp.float32) ** level_of(arg_keys[0], (PLANES, NY, NX), ((1, 8), (2, 4)), -0.2, 0.2), 0.5, 2.0)
    views_data = jnp.clip(jnp.exp(math.log(4.0) - 2.7725887 * jax.random.uniform(arg_keys[1], (VIEWS, PLANES, NY, NX), jnp.float32) ** level_of(arg_keys[1], (VIEWS, PLANES, NY, NX), ((2, 8), (3, 4)), -0.2, 0.2)), 0.25, 4.0).astype(jnp.bfloat16)
    psf_rows = jnp.clip(jnp.exp(jax.random.uniform(arg_keys[2], (VIEWS, KW), jnp.float32, math.log(0.05), math.log(1.0))), 0.05, 1.0)
    psf_cols = jnp.clip(jnp.exp(jax.random.uniform(arg_keys[3], (VIEWS, KW), jnp.float32, math.log(0.05), math.log(1.0))), 0.05, 1.0)
    return dict(estimate=estimate, views_data=views_data, psf_rows=psf_rows, psf_cols=psf_cols)


def blur_along(source, kernel, along_axis):
    reach = (kernel.shape[0] - 1) // 2
    lhs = source[:, None, :, :]
    if along_axis == 0:
        rhs = kernel.reshape(1, 1, kernel.shape[0], 1)
        padding = ((reach, reach), (0, 0))
    else:
        rhs = kernel.reshape(1, 1, 1, kernel.shape[0])
        padding = ((0, 0), (reach, reach))
    result = lax.conv_general_dilated(lhs, rhs, (1, 1), padding, precision=lax.Precision.HIGHEST)
    return result[:, 0, :, :]


def reference(estimate, views_data, psf_rows, psf_cols):
    kernels_y = psf_rows / jnp.sum(psf_rows, axis=1, keepdims=True)
    kernels_x = psf_cols / jnp.sum(psf_cols, axis=1, keepdims=True)
    log_sum = jnp.zeros(estimate.shape, jnp.float32)
    for view_index in range(VIEWS):
        blurred = blur_along(blur_along(estimate, kernels_x[view_index], 1), kernels_y[view_index], 0)
        quotient = views_data[view_index].astype(jnp.float32) / blurred
        correction = blur_along(blur_along(quotient, kernels_x[view_index][::-1], 1), kernels_y[view_index][::-1], 0)
        log_sum = log_sum + jnp.log(correction)
    return estimate * jnp.exp(log_sum / VIEWS)
```

```python
import functools

import jax
import jax.numpy as jnp
from jax import lax
from jax.experimental import pallas as pl
from jax.experimental.pallas import tpu as pltpu
from jax.sharding import PartitionSpec as P

BF = jnp.bfloat16
F32 = jnp.float32
MESH = pl.DeviceIdType.MESH


def dot(a, b, contract_b=0):
    return lax.dot_general(
        a, b, (((1,), (contract_b,)), ((), ())), preferred_element_type=F32
    )


def kernel(
    nr, nc, reach,
    est_hbm, views_hbm, pr_hbm, pc_hbm, out_ref,
    est_v, views_v, vu, vd, pr_v, pc_v, kp, ky_s, kt_s, df_s, da_s,
    ext, ybuf, recip, edge, edge_l, edge_r, gbuf, gedge, gedge_l, gedge_r,
    local_sem, send_sem, recv_sem,
):
    views, planes, height, width = views_v.shape
    taps = pr_v.shape[1]
    inner = height + 2 * reach
    outer = height + 4 * reach
    per = width // (2 * reach)
    groups = planes // per
    r, c = lax.axis_index("row"), lax.axis_index("col")
    up, down = (r - 1, c), (r + 1, c)
    left, right = (r, c - 1), (r, c + 1)
    has_up, has_down, has_left, has_right = r > 0, r < nr - 1, c > 0, c < nc - 1
    sides = ((has_up, up), (has_down, down), (has_left, left), (has_right, right))

    local = [
        pltpu.make_async_copy(s, d, local_sem.at[i])
        for i, (s, d) in enumerate(
            ((est_hbm, est_v), (pr_hbm, pr_v), (pc_hbm, pc_v), (views_hbm, views_v))
        )
    ]
    for copy in local:
        copy.start()

    barrier = pltpu.get_barrier_semaphore()
    for has, where in sides:
        @pl.when(has)
        def _():
            pl.semaphore_signal(barrier, inc=1, device_id=where, device_id_type=MESH)

    def remote(src, dst, slot, where):
        return pltpu.make_async_remote_copy(
            src_ref=src, dst_ref=dst, send_sem=send_sem.at[slot],
            recv_sem=recv_sem.at[slot], device_id=where, device_id_type=MESH,
        )

    to_up = [
        remote(ext.at[1], ext.at[2], 1, up),
        remote(views_hbm.at[:, :, pl.ds(0, reach), :], vd, 3, up),
    ]
    to_down = [
        remote(ext.at[1], ext.at[0], 0, down),
        remote(views_hbm.at[:, :, pl.ds(height - reach, reach), :], vu, 2, down),
    ]
    to_left = [remote(edge, edge_r, 5, left), remote(gedge, gedge_r, 7, left)]
    to_right = [remote(edge, edge_l, 4, right), remote(gedge, gedge_l, 6, right)]

    def start(which):
        for has, copies in which:
            @pl.when(has)
            def _(copies=copies):
                copies.start()

    def arrive(which):
        for has, copies in which:
            @pl.when(has)
            def _(copies=copies):
                copies.wait_recv()

    local[0].wait()
    for p in range(planes):
        ext[1, :, p * width:(p + 1) * width] = est_v[p].astype(BF)
    peers = 0
    for has, where in sides:
        peers = peers + has.astype(jnp.int32)
    pl.semaphore_wait(barrier, peers)
    start(((has_up, to_up[0]), (has_down, to_down[0])))
    start(((has_up, to_up[1]), (has_down, to_down[1])))

    for has, refs in (
        (has_up, (ext.at[0], vu)), (has_down, (ext.at[2], vd)),
        (has_left, (edge_l, gedge_l)), (has_right, (edge_r, gedge_r)),
    ):
        @pl.when(jnp.logical_not(has))
        def _(refs=refs):
            for ref in refs:
                ref[...] = jnp.zeros(ref.shape, ref.dtype)

    local[1].wait()
    local[2].wait()
    kp[...] = jnp.zeros(kp.shape, F32)
    psf_y, psf_x = pr_v[...], pc_v[...]
    kp[0:views, 0:taps] = psf_y / jnp.sum(psf_y, axis=1, keepdims=True)
    kp[views:2 * views, 0:taps] = psf_x / jnp.sum(psf_x, axis=1, keepdims=True)
    square = (width, width)
    apart = lax.broadcasted_iota(jnp.int32, square, 1) - lax.broadcasted_iota(jnp.int32, square, 0)
    near = (apart <= reach) & (apart >= -reach)
    for v in range(views):
        rows_y = jnp.broadcast_to(kp[v:v + 1, :], square)
        by = pltpu.roll(rows_y, 0, 1, stride=1, stride_axis=0)
        ky_s[v * inner:(v + 1) * inner, :] = by[:inner, :outer].astype(BF)
        kt_s[v] = by.T[2 * reach:2 * reach + height, :inner].astype(BF)
        rows_x = jnp.broadcast_to(kp[views + v:views + v + 1, :], square)
        bx = pltpu.roll(rows_x, width - reach, 1, stride=1, stride_axis=0)
        core = jnp.where(near, bx, 0.0).astype(BF)
        off = jnp.where(near, 0.0, bx).astype(BF)
        df_s[v, :, :width] = core
        df_s[v, :, width:] = off
        da_s[v, :width, :] = core
        da_s[v, width:, :] = off

    lane = lax.broadcasted_iota(jnp.int32, (8, width), 1)
    slot_of = ((lane + reach) // (2 * reach)) % per
    from_right = (lane // reach) % 2 == 0

    def mask(m, rows):
        return jnp.broadcast_to(m[:1], (rows, width))

    def pack(tiles):
        rows = tiles[0].shape[0]
        total = tiles[0]
        for k in range(1, per):
            total = jnp.where(mask(slot_of, rows) == k, pltpu.roll(tiles[k], 2 * reach * k, 1), total)
        return total

    arrive(((has_up, to_down[0]), (has_down, to_up[0])))
    e_all = ext[...].reshape(outer, planes * width)
    for g in range(groups):
        tiles = [
            e_all[:, (g * per + k) * width:(g * per + k + 1) * width].astype(F32)
            for k in range(per)
        ]
        edge[:, g * width:(g + 1) * width] = pack(tiles).astype(BF)
    start(((has_left, to_left[0]), (has_right, to_right[0])))
    ybuf[...] = dot(ky_s[...], e_all).astype(BF)
    arrive(((has_left, to_right[0]), (has_right, to_left[0])))
    sel = jnp.concatenate([mask(from_right, outer)] * groups, axis=1)
    edges = jnp.where(sel, edge_r[...].astype(F32), edge_l[...].astype(F32)).astype(BF)
    y_edges = dot(ky_s[...], edges)

    def unpack(tile, k):
        return tile if k == 0 else pltpu.roll(tile, width - 2 * reach * k, 1)

    row = lax.broadcasted_iota(jnp.int32, (inner, width), 0)
    inside = ((row >= reach) | has_up) & ((row < inner - reach) | has_down)
    for v in range(views):
        vs = slice(v * inner, (v + 1) * inner)
        parts = []
        for p in range(planes):
            g, k = divmod(p, per)
            halo = unpack(y_edges[vs, g * width:(g + 1) * width], k).astype(BF)
            parts.append(jnp.concatenate([ybuf[vs, p * width:(p + 1) * width], halo], axis=1))
        blurred = dot(jnp.concatenate(parts, axis=0), df_s[v], 1)
        for p in range(planes):
            b = blurred[p * inner:(p + 1) * inner]
            recip[v, p] = jnp.where(inside, 1.0 / b, 0.0)

    local[3].wait()
    arrive(((has_up, to_down[1]), (has_down, to_up[1])))
    for v in range(views):
        quot = []
        for p in range(planes):
            data = jnp.concatenate(
                [vu[v, p].astype(F32), views_v[v, p].astype(F32), vd[v, p].astype(F32)], axis=0
            )
            quot.append((data * recip[v, p]).astype(BF))
        g_v = dot(kt_s[v], jnp.concatenate(quot, axis=1))
        gbuf[v] = g_v
        for g in range(groups):
            tiles = [g_v[:, (g * per + k) * width:(g * per + k + 1) * width] for k in range(per)]
            gedge[v, :, g * width:(g + 1) * width] = pack(tiles).astype(BF)
    start(((has_left, to_left[1]), (has_right, to_right[1])))
    arrive(((has_left, to_right[1]), (has_right, to_left[1])))

    sel = jnp.concatenate([mask(from_right, height)] * groups, axis=1)
    product = None
    for v in range(views):
        halo = jnp.where(sel, gedge_r[v].astype(F32), gedge_l[v].astype(F32))
        parts, rest = [], []
        for p in range(planes):
            g, k = divmod(p, per)
            own = gbuf[v, :, p * width:(p + 1) * width]
            high = own.astype(BF)
            rest.append((own - high.astype(F32)).astype(BF))
            side = unpack(halo[:, g * width:(g + 1) * width], k).astype(BF)
            parts.append(jnp.concatenate([high, side], axis=1))
        corr = dot(jnp.concatenate(parts, axis=0), da_s[v])
        corr = corr + dot(jnp.concatenate(rest, axis=0), da_s[v, :width, :])
        product = corr if product is None else product * corr
    out_ref[...] = product.reshape(planes, height, width)

    for has, copies in ((has_up, to_up), (has_down, to_down), (has_left, to_left), (has_right, to_right)):
        @pl.when(has)
        def _(copies=copies):
            for copy in copies:
                copy.wait_send()


def local_step(nr, nc, estimate, views_data, psf_rows, psf_cols):
    views, planes, height, width = views_data.shape
    taps = psf_rows.shape[1]
    reach = (taps - 1) // 2
    inner, outer = height + 2 * reach, height + 4 * reach
    per = width // (2 * reach)
    groups = planes // per
    vm = pltpu.VMEM
    any_spec = pl.BlockSpec(memory_space=pl.ANY)
    product = pl.pallas_call(
        functools.partial(kernel, nr, nc, reach),
        out_shape=jax.ShapeDtypeStruct((planes, height, width), F32),
        in_specs=[any_spec] * 4,
        out_specs=pl.BlockSpec(memory_space=pltpu.VMEM),
        scratch_shapes=[
            vm((planes, height, width), F32),
            vm((views, planes, height, width), BF),
            vm((views, planes, reach, width), BF),
            vm((views, planes, reach, width), BF),
            vm((views, taps), F32),
            vm((views, taps), F32),
            vm((2 * views, width), F32),
            vm((views * inner, outer), BF),
            vm((views, height, inner), BF),
            vm((views, width, 2 * width), BF),
            vm((views, 2 * width, width), BF),
            vm((3, height, planes * width), BF),
            vm((views * inner, planes * width), BF),
            vm((views, planes, inner, width), F32),
            vm((outer, groups * width), BF),
            vm((outer, groups * width), BF),
            vm((outer, groups * width), BF),
            vm((views, height, planes * width), F32),
            vm((views, height, groups * width), BF),
            vm((views, height, groups * width), BF),
            vm((views, height, groups * width), BF),
            pltpu.SemaphoreType.DMA((4,)),
            pltpu.SemaphoreType.DMA((8,)),
            pltpu.SemaphoreType.DMA((8,)),
        ],
        compiler_params=pltpu.CompilerParams(
            collective_id=0, has_side_effects=True, vmem_limit_bytes=32 * 1024 * 1024
        ),
        name="deconvolve",
    )(estimate, views_data, psf_rows, psf_cols)
    return estimate * jnp.sqrt(jnp.sqrt(product))


def solution(mesh):
    nr, nc = mesh.shape["row"], mesh.shape["col"]
    return jax.shard_map(
        functools.partial(local_step, nr, nc),
        mesh=mesh,
        in_specs=(P(None, "row", "col"), P(None, None, "row", "col"), P(), P()),
        out_specs=P(None, "row", "col"),
        check_vma=False,
    )
```

```python
import functools

import jax
import jax.numpy as jnp
from jax import lax
from jax.experimental import pallas as pl
from jax.experimental.pallas import tpu as pltpu
from jax.sharding import PartitionSpec as P

BF = jnp.bfloat16
F32 = jnp.float32
MESH = pl.DeviceIdType.MESH


def dot(a, b, contract_b=0):
    return lax.dot_general(
        a, b, (((1,), (contract_b,)), ((), ())), preferred_element_type=F32
    )


def kernel(
    nr, nc, reach,
    est_hbm, views_hbm, pr_hbm, pc_hbm, out_ref,
    est_v, views_v, vu, vd, pr_v, pc_v, kp, ky_s, kt_s, df_s, da_s,
    ext, ybuf, recip, edge, edge_l, edge_r, gbuf, gedge, gedge_l, gedge_r,
    local_sem, send_sem, recv_sem,
):
    views, planes, height, width = views_v.shape
    taps = pr_v.shape[1]
    inner = height + 2 * reach
    outer = height + 4 * reach
    per = width // (2 * reach)
    groups = planes // per
    r, c = lax.axis_index("row"), lax.axis_index("col")
    up, down = (r - 1, c), (r + 1, c)
    left, right = (r, c - 1), (r, c + 1)
    has_up, has_down, has_left, has_right = r > 0, r < nr - 1, c > 0, c < nc - 1
    sides = ((has_up, up), (has_down, down), (has_left, left), (has_right, right))

    local = [
        pltpu.make_async_copy(s, d, local_sem.at[i])
        for i, (s, d) in enumerate(
            ((est_hbm, est_v), (pr_hbm, pr_v), (pc_hbm, pc_v), (views_hbm, views_v))
        )
    ]
    for copy in local:
        copy.start()

    barrier = pltpu.get_barrier_semaphore()
    for has, where in sides:
        @pl.when(has)
        def _():
            pl.semaphore_signal(barrier, inc=1, device_id=where, device_id_type=MESH)

    def remote(src, dst, slot, where):
        return pltpu.make_async_remote_copy(
            src_ref=src, dst_ref=dst, send_sem=send_sem.at[slot],
            recv_sem=recv_sem.at[slot], device_id=where, device_id_type=MESH,
        )

    views_at, gedge_at = 4, 4 + 2 * views
    to_up = [
        remote(ext.at[1], ext.at[2], 1, up),
    ] + [
        remote(views_hbm.at[v, :, pl.ds(0, reach), :], vd.at[v], views_at + views + v, up)
        for v in range(views)
    ]
    to_down = [
        remote(ext.at[1], ext.at[0], 0, down),
    ] + [
        remote(views_hbm.at[v, :, pl.ds(height - reach, reach), :], vu.at[v], views_at + v, down)
        for v in range(views)
    ]
    to_left = [remote(edge, edge_r, 3, left)] + [
        remote(gedge.at[v], gedge_r.at[v], gedge_at + views + v, left) for v in range(views)
    ]
    to_right = [remote(edge, edge_l, 2, right)] + [
        remote(gedge.at[v], gedge_l.at[v], gedge_at + v, right) for v in range(views)
    ]

    def start(which):
        for has, copies in which:
            @pl.when(has)
            def _(copies=copies):
                copies.start()

    def arrive(which):
        for has, copies in which:
            @pl.when(has)
            def _(copies=copies):
                copies.wait_recv()

    local[0].wait()
    for p in range(planes):
        ext[1, :, p * width:(p + 1) * width] = est_v[p].astype(BF)
    peers = 0
    for has, where in sides:
        peers = peers + has.astype(jnp.int32)
    pl.semaphore_wait(barrier, peers)
    start(((has_up, to_up[0]), (has_down, to_down[0])))
    for v in range(views):
        start(((has_up, to_up[1 + v]), (has_down, to_down[1 + v])))

    for has, refs in (
        (has_up, (ext.at[0], vu)), (has_down, (ext.at[2], vd)),
        (has_left, (edge_l, gedge_l)), (has_right, (edge_r, gedge_r)),
    ):
        @pl.when(jnp.logical_not(has))
        def _(refs=refs):
            for ref in refs:
                ref[...] = jnp.zeros(ref.shape, ref.dtype)

    local[1].wait()
    local[2].wait()
    kp[...] = jnp.zeros(kp.shape, F32)
    psf_y, psf_x = pr_v[...], pc_v[...]
    kp[0:views, 0:taps] = psf_y / jnp.sum(psf_y, axis=1, keepdims=True)
    kp[views:2 * views, 0:taps] = psf_x / jnp.sum(psf_x, axis=1, keepdims=True)
    square = (width, width)
    apart = lax.broadcasted_iota(jnp.int32, square, 1) - lax.broadcasted_iota(jnp.int32, square, 0)
    near = (apart <= reach) & (apart >= -reach)
    for v in range(views):
        rows_y = jnp.broadcast_to(kp[v:v + 1, :], square)
        by = pltpu.roll(rows_y, 0, 1, stride=1, stride_axis=0)
        ky_s[v * inner:(v + 1) * inner, :] = by[:inner, :outer].astype(BF)
        kt_s[v] = by.T[2 * reach:2 * reach + height, :inner].astype(BF)
        rows_x = jnp.broadcast_to(kp[views + v:views + v + 1, :], square)
        bx = pltpu.roll(rows_x, width - reach, 1, stride=1, stride_axis=0)
        core = jnp.where(near, bx, 0.0).astype(BF)
        off = jnp.where(near, 0.0, bx).astype(BF)
        df_s[v, :, :width] = core
        df_s[v, :, width:] = off
        da_s[v, :width, :] = core
        da_s[v, width:, :] = off

    lane = lax.broadcasted_iota(jnp.int32, (8, width), 1)
    slot_of = ((lane + reach) // (2 * reach)) % per
    from_right = (lane // reach) % 2 == 0

    def mask(m, rows):
        return jnp.broadcast_to(m[:1], (rows, width))

    def pack(tiles):
        rows = tiles[0].shape[0]
        total = tiles[0]
        for k in range(1, per):
            total = jnp.where(mask(slot_of, rows) == k, pltpu.roll(tiles[k], 2 * reach * k, 1), total)
        return total

    arrive(((has_up, to_down[0]), (has_down, to_up[0])))
    e_all = ext[...].reshape(outer, planes * width)
    for g in range(groups):
        tiles = [
            e_all[:, (g * per + k) * width:(g * per + k + 1) * width].astype(F32)
            for k in range(per)
        ]
        edge[:, g * width:(g + 1) * width] = pack(tiles).astype(BF)
    start(((has_left, to_left[0]), (has_right, to_right[0])))
    ybuf[...] = dot(ky_s[...], e_all).astype(BF)
    arrive(((has_left, to_right[0]), (has_right, to_left[0])))
    sel = jnp.concatenate([mask(from_right, outer)] * groups, axis=1)
    edges = jnp.where(sel, edge_r[...].astype(F32), edge_l[...].astype(F32)).astype(BF)
    y_edges = dot(ky_s[...], edges)

    def unpack(tile, k):
        return tile if k == 0 else pltpu.roll(tile, width - 2 * reach * k, 1)

    row = lax.broadcasted_iota(jnp.int32, (inner, width), 0)
    inside = ((row >= reach) | has_up) & ((row < inner - reach) | has_down)
    for v in range(views):
        vs = slice(v * inner, (v + 1) * inner)
        parts = []
        for p in range(planes):
            g, k = divmod(p, per)
            halo = unpack(y_edges[vs, g * width:(g + 1) * width], k).astype(BF)
            parts.append(jnp.concatenate([ybuf[vs, p * width:(p + 1) * width], halo], axis=1))
        blurred = dot(jnp.concatenate(parts, axis=0), df_s[v], 1)
        for p in range(planes):
            b = blurred[p * inner:(p + 1) * inner]
            recip[v, p] = jnp.where(inside, 1.0 / b, 0.0)

    sel = jnp.concatenate([mask(from_right, height)] * groups, axis=1)

    def send_edges(v):
        arrive(((has_up, to_down[1 + v]), (has_down, to_up[1 + v])))
        quot = []
        for p in range(planes):
            data = jnp.concatenate(
                [vu[v, p].astype(F32), views_v[v, p].astype(F32), vd[v, p].astype(F32)], axis=0
            )
            quot.append((data * recip[v, p]).astype(BF))
        g_v = dot(kt_s[v], jnp.concatenate(quot, axis=1))
        gbuf[v] = g_v
        for g in range(groups):
            tiles = [g_v[:, (g * per + k) * width:(g * per + k + 1) * width] for k in range(per)]
            gedge[v, :, g * width:(g + 1) * width] = pack(tiles).astype(BF)
        start(((has_left, to_left[1 + v]), (has_right, to_right[1 + v])))

    def corrected(v):
        arrive(((has_left, to_right[1 + v]), (has_right, to_left[1 + v])))
        halo = jnp.where(sel, gedge_r[v].astype(F32), gedge_l[v].astype(F32))
        parts, rest = [], []
        for p in range(planes):
            g, k = divmod(p, per)
            own = gbuf[v, :, p * width:(p + 1) * width]
            high = own.astype(BF)
            rest.append((own - high.astype(F32)).astype(BF))
            side = unpack(halo[:, g * width:(g + 1) * width], k).astype(BF)
            parts.append(jnp.concatenate([high, side], axis=1))
        corr = dot(jnp.concatenate(parts, axis=0), da_s[v])
        corr = corr + dot(jnp.concatenate(rest, axis=0), da_s[v, :width, :])
        corr = corr.reshape(planes, height, width)
        out_ref[...] = corr if v == 0 else out_ref[...] * corr

    local[3].wait()
    for v in range(views):
        send_edges(v)
        if v > 0:
            corrected(v - 1)
    corrected(views - 1)

    for has, copies in ((has_up, to_up), (has_down, to_down), (has_left, to_left), (has_right, to_right)):
        @pl.when(has)
        def _(copies=copies):
            for copy in copies:
                copy.wait_send()


def local_step(nr, nc, estimate, views_data, psf_rows, psf_cols):
    views, planes, height, width = views_data.shape
    taps = psf_rows.shape[1]
    reach = (taps - 1) // 2
    inner, outer = height + 2 * reach, height + 4 * reach
    per = width // (2 * reach)
    groups = planes // per
    vm = pltpu.VMEM
    any_spec = pl.BlockSpec(memory_space=pltpu.HBM)
    product = pl.pallas_call(
        functools.partial(kernel, nr, nc, reach),
        out_shape=jax.ShapeDtypeStruct((planes, height, width), F32),
        in_specs=[any_spec] * 4,
        out_specs=pl.BlockSpec(memory_space=pltpu.VMEM),
        scratch_shapes=[
            vm((planes, height, width), F32),
            vm((views, planes, height, width), BF),
            vm((views, planes, reach, width), BF),
            vm((views, planes, reach, width), BF),
            vm((views, taps), F32),
            vm((views, taps), F32),
            vm((2 * views, width), F32),
            vm((views * inner, outer), BF),
            vm((views, height, inner), BF),
            vm((views, width, 2 * width), BF),
            vm((views, 2 * width, width), BF),
            vm((3, height, planes * width), BF),
            vm((views * inner, planes * width), BF),
            vm((views, planes, inner, width), F32),
            vm((outer, groups * width), BF),
            vm((outer, groups * width), BF),
            vm((outer, groups * width), BF),
            vm((views, height, planes * width), F32),
            vm((views, height, groups * width), BF),
            vm((views, height, groups * width), BF),
            vm((views, height, groups * width), BF),
            pltpu.SemaphoreType.DMA((4,)),
            pltpu.SemaphoreType.DMA((4 + 4 * views,)),
            pltpu.SemaphoreType.DMA((4 + 4 * views,)),
        ],
        compiler_params=pltpu.CompilerParams(
            collective_id=0, has_side_effects=True, vmem_limit_bytes=48 * 1024 * 1024
        ),
        name="deconvolve",
    )(estimate, views_data, psf_rows, psf_cols)
    return estimate * jnp.sqrt(jnp.sqrt(product))


def solution(mesh):
    nr, nc = mesh.shape["row"], mesh.shape["col"]
    return jax.shard_map(
        functools.partial(local_step, nr, nc),
        mesh=mesh,
        in_specs=(P(None, "row", "col"), P(None, None, "row", "col"), P(), P()),
        out_specs=P(None, "row", "col"),
        check_vma=False,
    )
```

```python
import functools

import jax
import jax.numpy as jnp
from jax import lax
from jax.experimental import pallas as pl
from jax.experimental.pallas import tpu as pltpu
from jax.sharding import PartitionSpec as P

BF = jnp.bfloat16
F32 = jnp.float32
MESH = pl.DeviceIdType.MESH


def dot(a, b, contract_b=0):
    return lax.dot_general(
        a, b, (((1,), (contract_b,)), ((), ())), preferred_element_type=F32
    )


def kernel(
    nr, nc, reach,
    est_hbm, views_hbm, pr_hbm, pc_hbm, out_ref,
    est_v, views_v, vu, vd, pr_v, pc_v, kp, ky_s, kt_s, df_s, da_s,
    ext, ybuf, recip, edge, edge_l, edge_r, gbuf, gedge, gedge_l, gedge_r,
    local_sem, send_sem, recv_sem,
):
    views, planes, height, width = views_v.shape
    taps = pr_v.shape[1]
    inner = height + 2 * reach
    outer = height + 4 * reach
    per = width // (2 * reach)
    groups = planes // per
    r, c = lax.axis_index("row"), lax.axis_index("col")
    up, down = (r - 1, c), (r + 1, c)
    left, right = (r, c - 1), (r, c + 1)
    has_up, has_down, has_left, has_right = r > 0, r < nr - 1, c > 0, c < nc - 1
    sides = ((has_up, up), (has_down, down), (has_left, left), (has_right, right))

    local = [
        pltpu.make_async_copy(s, d, local_sem.at[i])
        for i, (s, d) in enumerate(
            ((est_hbm, est_v), (pr_hbm, pr_v), (pc_hbm, pc_v), (views_hbm, views_v))
        )
    ]
    for copy in local:
        copy.start()

    barrier = pltpu.get_barrier_semaphore()
    for has, where in sides:
        @pl.when(has)
        def _():
            pl.semaphore_signal(barrier, inc=1, device_id=where, device_id_type=MESH)

    def remote(src, dst, slot, where):
        return pltpu.make_async_remote_copy(
            src_ref=src, dst_ref=dst, send_sem=send_sem.at[slot],
            recv_sem=recv_sem.at[slot], device_id=where, device_id_type=MESH,
        )

    views_at, gedge_at = 4, 4 + 2 * views
    to_up = [
        remote(ext.at[1], ext.at[2], 1, up),
    ] + [
        remote(views_v.at[v, :, pl.ds(0, reach), :], vd.at[v], views_at + views + v, up)
        for v in range(views)
    ]
    to_down = [
        remote(ext.at[1], ext.at[0], 0, down),
    ] + [
        remote(views_v.at[v, :, pl.ds(height - reach, reach), :], vu.at[v], views_at + v, down)
        for v in range(views)
    ]
    to_left = [remote(edge, edge_r, 3, left)] + [
        remote(gedge.at[v], gedge_r.at[v], gedge_at + views + v, left) for v in range(views)
    ]
    to_right = [remote(edge, edge_l, 2, right)] + [
        remote(gedge.at[v], gedge_l.at[v], gedge_at + v, right) for v in range(views)
    ]

    def start(which):
        for has, copies in which:
            @pl.when(has)
            def _(copies=copies):
                copies.start()

    def arrive(which):
        for has, copies in which:
            @pl.when(has)
            def _(copies=copies):
                copies.wait_recv()

    local[0].wait()
    for p in range(planes):
        ext[1, :, p * width:(p + 1) * width] = est_v[p].astype(BF)
    peers = 0
    for has, where in sides:
        peers = peers + has.astype(jnp.int32)
    pl.semaphore_wait(barrier, peers)
    start(((has_up, to_up[0]), (has_down, to_down[0])))
    local[3].wait()
    for v in range(views):
        start(((has_up, to_up[1 + v]), (has_down, to_down[1 + v])))

    for has, refs in (
        (has_up, (ext.at[0], vu)), (has_down, (ext.at[2], vd)),
        (has_left, (edge_l, gedge_l)), (has_right, (edge_r, gedge_r)),
    ):
        @pl.when(jnp.logical_not(has))
        def _(refs=refs):
            for ref in refs:
                ref[...] = jnp.zeros(ref.shape, ref.dtype)

    local[1].wait()
    local[2].wait()
    kp[...] = jnp.zeros(kp.shape, F32)
    psf_y, psf_x = pr_v[...], pc_v[...]
    kp[0:views, 0:taps] = psf_y / jnp.sum(psf_y, axis=1, keepdims=True)
    kp[views:2 * views, 0:taps] = psf_x / jnp.sum(psf_x, axis=1, keepdims=True)
    square = (width, width)
    apart = lax.broadcasted_iota(jnp.int32, square, 1) - lax.broadcasted_iota(jnp.int32, square, 0)
    near = (apart <= reach) & (apart >= -reach)
    for v in range(views):
        rows_y = jnp.broadcast_to(kp[v:v + 1, :], square)
        by = pltpu.roll(rows_y, 0, 1, stride=1, stride_axis=0)
        ky_s[v * inner:(v + 1) * inner, :] = by[:inner, :outer].astype(BF)
        kt_s[v] = by.T[2 * reach:2 * reach + height, :inner].astype(BF)
        rows_x = jnp.broadcast_to(kp[views + v:views + v + 1, :], square)
        bx = pltpu.roll(rows_x, width - reach, 1, stride=1, stride_axis=0)
        core = jnp.where(near, bx, 0.0).astype(BF)
        off = jnp.where(near, 0.0, bx).astype(BF)
        df_s[v, :, :width] = core
        df_s[v, :, width:] = off
        da_s[v, :width, :] = core
        da_s[v, width:, :] = off

    lane = lax.broadcasted_iota(jnp.int32, (8, width), 1)
    slot_of = ((lane + reach) // (2 * reach)) % per
    from_right = (lane // reach) % 2 == 0

    def mask(m, rows):
        return jnp.broadcast_to(m[:1], (rows, width))

    def pack(tiles):
        rows = tiles[0].shape[0]
        total = tiles[0]
        for k in range(1, per):
            total = jnp.where(mask(slot_of, rows) == k, pltpu.roll(tiles[k], 2 * reach * k, 1), total)
        return total

    arrive(((has_up, to_down[0]), (has_down, to_up[0])))
    e_all = ext[...].reshape(outer, planes * width)
    for g in range(groups):
        tiles = [
            e_all[:, (g * per + k) * width:(g * per + k + 1) * width].astype(F32)
            for k in range(per)
        ]
        edge[:, g * width:(g + 1) * width] = pack(tiles).astype(BF)
    start(((has_left, to_left[0]), (has_right, to_right[0])))
    ybuf[...] = dot(ky_s[...], e_all).astype(BF)
    arrive(((has_left, to_right[0]), (has_right, to_left[0])))
    sel = jnp.concatenate([mask(from_right, outer)] * groups, axis=1)
    edges = jnp.where(sel, edge_r[...].astype(F32), edge_l[...].astype(F32)).astype(BF)
    y_edges = dot(ky_s[...], edges)

    def unpack(tile, k):
        return tile if k == 0 else pltpu.roll(tile, width - 2 * reach * k, 1)

    row = lax.broadcasted_iota(jnp.int32, (inner, width), 0)
    inside = ((row >= reach) | has_up) & ((row < inner - reach) | has_down)
    for v in range(views):
        vs = slice(v * inner, (v + 1) * inner)
        parts = []
        for p in range(planes):
            g, k = divmod(p, per)
            halo = unpack(y_edges[vs, g * width:(g + 1) * width], k).astype(BF)
            parts.append(jnp.concatenate([ybuf[vs, p * width:(p + 1) * width], halo], axis=1))
        blurred = dot(jnp.concatenate(parts, axis=0), df_s[v], 1)
        for p in range(planes):
            b = blurred[p * inner:(p + 1) * inner]
            recip[v, p] = jnp.where(inside, 1.0 / b, 0.0)

    sel = jnp.concatenate([mask(from_right, height)] * groups, axis=1)

    def send_edges(v):
        arrive(((has_up, to_down[1 + v]), (has_down, to_up[1 + v])))
        quot = []
        for p in range(planes):
            data = jnp.concatenate(
                [vu[v, p].astype(F32), views_v[v, p].astype(F32), vd[v, p].astype(F32)], axis=0
            )
            quot.append((data * recip[v, p]).astype(BF))
        g_v = dot(kt_s[v], jnp.concatenate(quot, axis=1))
        gbuf[v] = g_v
        for g in range(groups):
            tiles = [g_v[:, (g * per + k) * width:(g * per + k + 1) * width] for k in range(per)]
            gedge[v, :, g * width:(g + 1) * width] = pack(tiles).astype(BF)
        start(((has_left, to_left[1 + v]), (has_right, to_right[1 + v])))

    def corrected(v):
        arrive(((has_left, to_right[1 + v]), (has_right, to_left[1 + v])))
        halo = jnp.where(sel, gedge_r[v].astype(F32), gedge_l[v].astype(F32))
        parts, rest = [], []
        for p in range(planes):
            g, k = divmod(p, per)
            own = gbuf[v, :, p * width:(p + 1) * width]
            high = own.astype(BF)
            rest.append((own - high.astype(F32)).astype(BF))
            side = unpack(halo[:, g * width:(g + 1) * width], k).astype(BF)
            parts.append(jnp.concatenate([high, side], axis=1))
        corr = dot(jnp.concatenate(parts, axis=0), da_s[v])
        corr = corr + dot(jnp.concatenate(rest, axis=0), da_s[v, :width, :])
        corr = corr.reshape(planes, height, width)
        out_ref[...] = corr if v == 0 else out_ref[...] * corr

    for v in range(views):
        send_edges(v)
    for v in range(views):
        corrected(v)

    for has, copies in ((has_up, to_up), (has_down, to_down), (has_left, to_left), (has_right, to_right)):
        @pl.when(has)
        def _(copies=copies):
            for copy in copies:
                copy.wait_send()


def local_step(nr, nc, estimate, views_data, psf_rows, psf_cols):
    views, planes, height, width = views_data.shape
    taps = psf_rows.shape[1]
    reach = (taps - 1) // 2
    inner, outer = height + 2 * reach, height + 4 * reach
    per = width // (2 * reach)
    groups = planes // per
    vm = pltpu.VMEM
    any_spec = pl.BlockSpec(memory_space=pl.ANY)
    product = pl.pallas_call(
        functools.partial(kernel, nr, nc, reach),
        out_shape=jax.ShapeDtypeStruct((planes, height, width), F32),
        in_specs=[any_spec] * 4,
        out_specs=pl.BlockSpec(memory_space=pltpu.VMEM),
        scratch_shapes=[
            vm((planes, height, width), F32),
            vm((views, planes, height, width), BF),
            vm((views, planes, reach, width), BF),
            vm((views, planes, reach, width), BF),
            vm((views, taps), F32),
            vm((views, taps), F32),
            vm((2 * views, width), F32),
            vm((views * inner, outer), BF),
            vm((views, height, inner), BF),
            vm((views, width, 2 * width), BF),
            vm((views, 2 * width, width), BF),
            vm((3, height, planes * width), BF),
            vm((views * inner, planes * width), BF),
            vm((views, planes, inner, width), F32),
            vm((outer, groups * width), BF),
            vm((outer, groups * width), BF),
            vm((outer, groups * width), BF),
            vm((views, height, planes * width), F32),
            vm((views, height, groups * width), BF),
            vm((views, height, groups * width), BF),
            vm((views, height, groups * width), BF),
            pltpu.SemaphoreType.DMA((4,)),
            pltpu.SemaphoreType.DMA((4 + 4 * views,)),
            pltpu.SemaphoreType.DMA((4 + 4 * views,)),
        ],
        compiler_params=pltpu.CompilerParams(collective_id=0, has_side_effects=True),
        name="deconvolve",
    )(estimate, views_data, psf_rows, psf_cols)
    return estimate * jnp.sqrt(jnp.sqrt(product))


def solution(mesh):
    nr, nc = mesh.shape["row"], mesh.shape["col"]
    return jax.shard_map(
        functools.partial(local_step, nr, nc),
        mesh=mesh,
        in_specs=(P(None, "row", "col"), P(None, None, "row", "col"), P(), P()),
        out_specs=P(None, "row", "col"),
        check_vma=False,
    )
```

```python
import functools

import jax
import jax.numpy as jnp
from jax import lax
from jax.experimental import pallas as pl
from jax.experimental.pallas import tpu as pltpu
from jax.sharding import PartitionSpec as P

BF = jnp.bfloat16
F32 = jnp.float32
MESH = pl.DeviceIdType.MESH


def dot(a, b, contract_b=0):
    return lax.dot_general(
        a, b, (((1,), (contract_b,)), ((), ())), preferred_element_type=F32
    )


def kernel(
    nr, nc, reach,
    est_hbm, views_hbm, pr_hbm, pc_hbm, out_ref,
    est_v, views_v, vu, vd, pr_v, pc_v, kp, ky_s, kt_s, df_s, da_s,
    ext, ybuf, recip, edge, edge_l, edge_r, gbuf, gedge, gedge_l, gedge_r,
    local_sem, send_sem, recv_sem,
):
    views, planes, height, width = views_v.shape
    taps = pr_v.shape[1]
    inner = height + 2 * reach
    outer = height + 4 * reach
    per = width // (2 * reach)
    groups = planes // per
    r, c = lax.axis_index("row"), lax.axis_index("col")
    up, down = (r - 1, c), (r + 1, c)
    left, right = (r, c - 1), (r, c + 1)
    has_up, has_down, has_left, has_right = r > 0, r < nr - 1, c > 0, c < nc - 1
    sides = ((has_up, up), (has_down, down), (has_left, left), (has_right, right))

    local = [
        pltpu.make_async_copy(s, d, local_sem.at[i])
        for i, (s, d) in enumerate(
            ((est_hbm, est_v), (pr_hbm, pr_v), (pc_hbm, pc_v), (views_hbm, views_v))
        )
    ]
    for copy in local:
        copy.start()

    barrier = pltpu.get_barrier_semaphore()
    for has, where in sides:
        @pl.when(has)
        def _():
            pl.semaphore_signal(barrier, inc=1, device_id=where, device_id_type=MESH)

    def remote(src, dst, slot, where):
        return pltpu.make_async_remote_copy(
            src_ref=src, dst_ref=dst, send_sem=send_sem.at[slot],
            recv_sem=recv_sem.at[slot], device_id=where, device_id_type=MESH,
        )

    views_at, gedge_at = 4, 4 + 2 * views
    to_up = [
        remote(ext.at[1], ext.at[2], 1, up),
    ] + [
        remote(views_v.at[v, :, pl.ds(0, reach), :], vd.at[v], views_at + views + v, up)
        for v in range(views)
    ]
    to_down = [
        remote(ext.at[1], ext.at[0], 0, down),
    ] + [
        remote(views_v.at[v, :, pl.ds(height - reach, reach), :], vu.at[v], views_at + v, down)
        for v in range(views)
    ]
    to_left = [remote(edge, edge_r, 3, left)] + [
        remote(gedge.at[v], gedge_r.at[v], gedge_at + views + v, left) for v in range(views)
    ]
    to_right = [remote(edge, edge_l, 2, right)] + [
        remote(gedge.at[v], gedge_l.at[v], gedge_at + v, right) for v in range(views)
    ]

    def start(which):
        for has, copies in which:
            @pl.when(has)
            def _(copies=copies):
                copies.start()

    def arrive(which):
        for has, copies in which:
            @pl.when(has)
            def _(copies=copies):
                copies.wait_recv()

    local[0].wait()
    for p in range(planes):
        ext[1, :, p * width:(p + 1) * width] = est_v[p].astype(BF)
    peers = 0
    for has, where in sides:
        peers = peers + has.astype(jnp.int32)
    pl.semaphore_wait(barrier, peers)
    start(((has_up, to_up[0]), (has_down, to_down[0])))
    for has, refs in (
        (has_up, (ext.at[0], vu)), (has_down, (ext.at[2], vd)),
        (has_left, (edge_l, gedge_l)), (has_right, (edge_r, gedge_r)),
    ):
        @pl.when(jnp.logical_not(has))
        def _(refs=refs):
            for ref in refs:
                ref[...] = jnp.zeros(ref.shape, ref.dtype)

    local[1].wait()
    local[2].wait()
    kp[...] = jnp.zeros(kp.shape, F32)
    psf_y, psf_x = pr_v[...], pc_v[...]
    kp[0:views, 0:taps] = psf_y / jnp.sum(psf_y, axis=1, keepdims=True)
    kp[views:2 * views, 0:taps] = psf_x / jnp.sum(psf_x, axis=1, keepdims=True)
    square = (width, width)
    apart = lax.broadcasted_iota(jnp.int32, square, 1) - lax.broadcasted_iota(jnp.int32, square, 0)
    near = (apart <= reach) & (apart >= -reach)
    for v in range(views):
        rows_y = jnp.broadcast_to(kp[v:v + 1, :], square)
        by = pltpu.roll(rows_y, 0, 1, stride=1, stride_axis=0)
        ky_s[v * inner:(v + 1) * inner, :] = by[:inner, :outer].astype(BF)
        kt_s[v] = by.T[2 * reach:2 * reach + height, :inner].astype(BF)
        rows_x = jnp.broadcast_to(kp[views + v:views + v + 1, :], square)
        bx = pltpu.roll(rows_x, width - reach, 1, stride=1, stride_axis=0)
        core = jnp.where(near, bx, 0.0).astype(BF)
        off = jnp.where(near, 0.0, bx).astype(BF)
        df_s[v, :, :width] = core
        df_s[v, :, width:] = off
        da_s[v, :width, :] = core
        da_s[v, width:, :] = off

    lane = lax.broadcasted_iota(jnp.int32, (8, width), 1)
    slot_of = ((lane + reach) // (2 * reach)) % per
    from_right = (lane // reach) % 2 == 0

    def mask(m, rows):
        return jnp.broadcast_to(m[:1], (rows, width))

    def pack(tiles):
        rows = tiles[0].shape[0]
        total = tiles[0]
        for k in range(1, per):
            total = jnp.where(mask(slot_of, rows) == k, pltpu.roll(tiles[k], 2 * reach * k, 1), total)
        return total

    local[3].wait()
    for has, copies in ((has_up, to_up), (has_down, to_down)):
        @pl.when(has)
        def _(copies=copies):
            copies[0].wait_send()
    for v in range(views):
        start(((has_up, to_up[1 + v]), (has_down, to_down[1 + v])))

    arrive(((has_up, to_down[0]), (has_down, to_up[0])))
    e_all = ext[...].reshape(outer, planes * width)
    for g in range(groups):
        tiles = [
            e_all[:, (g * per + k) * width:(g * per + k + 1) * width].astype(F32)
            for k in range(per)
        ]
        edge[:, g * width:(g + 1) * width] = pack(tiles).astype(BF)
    start(((has_left, to_left[0]), (has_right, to_right[0])))
    ybuf[...] = dot(ky_s[...], e_all).astype(BF)
    arrive(((has_left, to_right[0]), (has_right, to_left[0])))
    sel = jnp.concatenate([mask(from_right, outer)] * groups, axis=1)
    edges = jnp.where(sel, edge_r[...].astype(F32), edge_l[...].astype(F32)).astype(BF)
    y_edges = dot(ky_s[...], edges)

    def unpack(tile, k):
        return tile if k == 0 else pltpu.roll(tile, width - 2 * reach * k, 1)

    row = lax.broadcasted_iota(jnp.int32, (inner, width), 0)
    inside = ((row >= reach) | has_up) & ((row < inner - reach) | has_down)
    for v in range(views):
        vs = slice(v * inner, (v + 1) * inner)
        parts = []
        for p in range(planes):
            g, k = divmod(p, per)
            halo = unpack(y_edges[vs, g * width:(g + 1) * width], k).astype(BF)
            parts.append(jnp.concatenate([ybuf[vs, p * width:(p + 1) * width], halo], axis=1))
        blurred = dot(jnp.concatenate(parts, axis=0), df_s[v], 1)
        for p in range(planes):
            b = blurred[p * inner:(p + 1) * inner]
            recip[v, p] = jnp.where(inside, 1.0 / b, 0.0)

    sel = jnp.concatenate([mask(from_right, height)] * groups, axis=1)

    def send_edges(v):
        arrive(((has_up, to_down[1 + v]), (has_down, to_up[1 + v])))
        quot = []
        for p in range(planes):
            data = jnp.concatenate(
                [vu[v, p].astype(F32), views_v[v, p].astype(F32), vd[v, p].astype(F32)], axis=0
            )
            quot.append((data * recip[v, p]).astype(BF))
        g_v = dot(kt_s[v], jnp.concatenate(quot, axis=1))
        gbuf[v] = g_v
        for g in range(groups):
            tiles = [g_v[:, (g * per + k) * width:(g * per + k + 1) * width] for k in range(per)]
            gedge[v, :, g * width:(g + 1) * width] = pack(tiles).astype(BF)
        start(((has_left, to_left[1 + v]), (has_right, to_right[1 + v])))

    def corrected(v):
        arrive(((has_left, to_right[1 + v]), (has_right, to_left[1 + v])))
        halo = jnp.where(sel, gedge_r[v].astype(F32), gedge_l[v].astype(F32))
        parts, rest = [], []
        for p in range(planes):
            g, k = divmod(p, per)
            own = gbuf[v, :, p * width:(p + 1) * width]
            high = own.astype(BF)
            rest.append((own - high.astype(F32)).astype(BF))
            side = unpack(halo[:, g * width:(g + 1) * width], k).astype(BF)
            parts.append(jnp.concatenate([high, side], axis=1))
        corr = dot(jnp.concatenate(parts, axis=0), da_s[v])
        corr = corr + dot(jnp.concatenate(rest, axis=0), da_s[v, :width, :])
        corr = corr.reshape(planes, height, width)
        out_ref[...] = corr if v == 0 else out_ref[...] * corr

    for v in range(views):
        if v == views - 1:
            corrected(0)
        send_edges(v)
    for v in range(1, views):
        corrected(v)

    for has, copies in (
        (has_up, to_up[1:]), (has_down, to_down[1:]), (has_left, to_left), (has_right, to_right)
    ):
        @pl.when(has)
        def _(copies=copies):
            for copy in copies:
                copy.wait_send()


def local_step(nr, nc, estimate, views_data, psf_rows, psf_cols):
    views, planes, height, width = views_data.shape
    taps = psf_rows.shape[1]
    reach = (taps - 1) // 2
    inner, outer = height + 2 * reach, height + 4 * reach
    per = width // (2 * reach)
    groups = planes // per
    vm = pltpu.VMEM
    any_spec = pl.BlockSpec(memory_space=pl.ANY)
    product = pl.pallas_call(
        functools.partial(kernel, nr, nc, reach),
        out_shape=jax.ShapeDtypeStruct((planes, height, width), F32),
        in_specs=[any_spec] * 4,
        out_specs=pl.BlockSpec(memory_space=pltpu.VMEM),
        scratch_shapes=[
            vm((planes, height, width), F32),
            vm((views, planes, height, width), BF),
            vm((views, planes, reach, width), BF),
            vm((views, planes, reach, width), BF),
            vm((views, taps), F32),
            vm((views, taps), F32),
            vm((2 * views, width), F32),
            vm((views * inner, outer), BF),
            vm((views, height, inner), BF),
            vm((views, width, 2 * width), BF),
            vm((views, 2 * width, width), BF),
            vm((3, height, planes * width), BF),
            vm((views * inner, planes * width), BF),
            vm((views, planes, inner, width), F32),
            vm((outer, groups * width), BF),
            vm((outer, groups * width), BF),
            vm((outer, groups * width), BF),
            vm((views, height, planes * width), F32),
            vm((views, height, groups * width), BF),
            vm((views, height, groups * width), BF),
            vm((views, height, groups * width), BF),
            pltpu.SemaphoreType.DMA((4,)),
            pltpu.SemaphoreType.DMA((4 + 4 * views,)),
            pltpu.SemaphoreType.DMA((4 + 4 * views,)),
        ],
        compiler_params=pltpu.CompilerParams(collective_id=0, has_side_effects=True),
        name="deconvolve",
    )(estimate, views_data, psf_rows, psf_cols)
    return estimate * jnp.sqrt(jnp.sqrt(product))


def solution(mesh):
    nr, nc = mesh.shape["row"], mesh.shape["col"]
    return jax.shard_map(
        functools.partial(local_step, nr, nc),
        mesh=mesh,
        in_specs=(P(None, "row", "col"), P(None, None, "row", "col"), P(), P()),
        out_specs=P(None, "row", "col"),
        check_vma=False,
    )
```

```python
import functools

import jax
import jax.numpy as jnp
from jax import lax
from jax.experimental import pallas as pl
from jax.experimental.pallas import tpu as pltpu
from jax.sharding import PartitionSpec as P

BF = jnp.bfloat16
F32 = jnp.float32
MESH = pl.DeviceIdType.MESH


def dot(a, b, contract_b=0):
    return lax.dot_general(
        a, b, (((1,), (contract_b,)), ((), ())), preferred_element_type=F32
    )


def kernel(
    nr, nc, reach,
    est_hbm, views_hbm, pr_hbm, pc_hbm, out_ref,
    est_v, views_v, vu, vd, pr_v, pc_v, kp, ky_s, kt_s, df_s, da_s,
    ext, ybuf, recip, edge, edge_l, edge_r, gbuf, gedge, gedge_l, gedge_r,
    local_sem, send_sem, recv_sem,
):
    views, planes, height, width = views_v.shape
    taps = pr_v.shape[1]
    inner = height + 2 * reach
    outer = height + 4 * reach
    per = width // (2 * reach)
    groups = planes // per
    r, c = lax.axis_index("row"), lax.axis_index("col")
    up, down = (r - 1, c), (r + 1, c)
    left, right = (r, c - 1), (r, c + 1)
    has_up, has_down, has_left, has_right = r > 0, r < nr - 1, c > 0, c < nc - 1
    sides = ((has_up, up), (has_down, down), (has_left, left), (has_right, right))

    local = [
        pltpu.make_async_copy(s, d, local_sem.at[i])
        for i, (s, d) in enumerate(
            ((est_hbm, est_v), (pr_hbm, pr_v), (pc_hbm, pc_v), (views_hbm, views_v))
        )
    ]
    for copy in local:
        copy.start()

    barrier = pltpu.get_barrier_semaphore()
    for has, where in sides:
        @pl.when(has)
        def _():
            pl.semaphore_signal(barrier, inc=1, device_id=where, device_id_type=MESH)

    def remote(src, dst, slot, where):
        return pltpu.make_async_remote_copy(
            src_ref=src, dst_ref=dst, send_sem=send_sem.at[slot],
            recv_sem=recv_sem.at[slot], device_id=where, device_id_type=MESH,
        )

    views_at, gedge_at = 4, 4 + 2 * views
    to_up = [
        remote(ext.at[1], ext.at[2], 1, up),
    ] + [
        remote(views_v.at[v, :, pl.ds(0, reach), :], vd.at[v], views_at + views + v, up)
        for v in range(views)
    ]
    to_down = [
        remote(ext.at[1], ext.at[0], 0, down),
    ] + [
        remote(views_v.at[v, :, pl.ds(height - reach, reach), :], vu.at[v], views_at + v, down)
        for v in range(views)
    ]
    to_left = [remote(edge, edge_r, 3, left)] + [
        remote(gedge.at[v], gedge_r.at[v], gedge_at + views + v, left) for v in range(views)
    ]
    to_right = [remote(edge, edge_l, 2, right)] + [
        remote(gedge.at[v], gedge_l.at[v], gedge_at + v, right) for v in range(views)
    ]

    def start(which):
        for has, copies in which:
            @pl.when(has)
            def _(copies=copies):
                copies.start()

    def arrive(which):
        for has, copies in which:
            @pl.when(has)
            def _(copies=copies):
                copies.wait_recv()

    local[0].wait()
    for p in range(planes):
        ext[1, :, p * width:(p + 1) * width] = est_v[p].astype(BF)
    peers = 0
    for has, where in sides:
        peers = peers + has.astype(jnp.int32)
    pl.semaphore_wait(barrier, peers)
    start(((has_up, to_up[0]), (has_down, to_down[0])))
    local[3].wait()
    start(((has_up, to_up[1]), (has_down, to_down[1])))
    for has, refs in (
        (has_up, (ext.at[0], vu)), (has_down, (ext.at[2], vd)),
        (has_left, (edge_l, gedge_l)), (has_right, (edge_r, gedge_r)),
    ):
        @pl.when(jnp.logical_not(has))
        def _(refs=refs):
            for ref in refs:
                ref[...] = jnp.zeros(ref.shape, ref.dtype)

    local[1].wait()
    local[2].wait()
    kp[...] = jnp.zeros(kp.shape, F32)
    psf_y, psf_x = pr_v[...], pc_v[...]
    kp[0:views, 0:taps] = psf_y / jnp.sum(psf_y, axis=1, keepdims=True)
    kp[views:2 * views, 0:taps] = psf_x / jnp.sum(psf_x, axis=1, keepdims=True)
    square = (width, width)
    apart = lax.broadcasted_iota(jnp.int32, square, 1) - lax.broadcasted_iota(jnp.int32, square, 0)
    near = (apart <= reach) & (apart >= -reach)
    for v in range(views):
        rows_y = jnp.broadcast_to(kp[v:v + 1, :], square)
        by = pltpu.roll(rows_y, 0, 1, stride=1, stride_axis=0)
        ky_s[v * inner:(v + 1) * inner, :] = by[:inner, :outer].astype(BF)
        kt_s[v] = by.T[2 * reach:2 * reach + height, :inner].astype(BF)
        rows_x = jnp.broadcast_to(kp[views + v:views + v + 1, :], square)
        bx = pltpu.roll(rows_x, width - reach, 1, stride=1, stride_axis=0)
        core = jnp.where(near, bx, 0.0).astype(BF)
        off = jnp.where(near, 0.0, bx).astype(BF)
        df_s[v, :, :width] = core
        df_s[v, :, width:] = off
        da_s[v, :width, :] = core
        da_s[v, width:, :] = off

    lane = lax.broadcasted_iota(jnp.int32, (8, width), 1)
    slot_of = ((lane + reach) // (2 * reach)) % per
    from_right = (lane // reach) % 2 == 0

    def mask(m, rows):
        return jnp.broadcast_to(m[:1], (rows, width))

    def pack(tiles):
        rows = tiles[0].shape[0]
        total = tiles[0]
        for k in range(1, per):
            total = jnp.where(mask(slot_of, rows) == k, pltpu.roll(tiles[k], 2 * reach * k, 1), total)
        return total

    arrive(((has_up, to_down[0]), (has_down, to_up[0])))
    e_all = ext[...].reshape(outer, planes * width)
    for g in range(groups):
        tiles = [
            e_all[:, (g * per + k) * width:(g * per + k + 1) * width].astype(F32)
            for k in range(per)
        ]
        edge[:, g * width:(g + 1) * width] = pack(tiles).astype(BF)
    start(((has_left, to_left[0]), (has_right, to_right[0])))
    for v in range(1, views):
        start(((has_up, to_up[1 + v]), (has_down, to_down[1 + v])))
    ybuf[...] = dot(ky_s[...], e_all).astype(BF)
    arrive(((has_left, to_right[0]), (has_right, to_left[0])))
    sel = jnp.concatenate([mask(from_right, outer)] * groups, axis=1)
    edges = jnp.where(sel, edge_r[...].astype(F32), edge_l[...].astype(F32)).astype(BF)
    y_edges = dot(ky_s[...], edges)

    def unpack(tile, k):
        return tile if k == 0 else pltpu.roll(tile, width - 2 * reach * k, 1)

    row = lax.broadcasted_iota(jnp.int32, (inner, width), 0)
    inside = ((row >= reach) | has_up) & ((row < inner - reach) | has_down)
    for v in range(views):
        vs = slice(v * inner, (v + 1) * inner)
        parts = []
        for p in range(planes):
            g, k = divmod(p, per)
            halo = unpack(y_edges[vs, g * width:(g + 1) * width], k).astype(BF)
            parts.append(jnp.concatenate([ybuf[vs, p * width:(p + 1) * width], halo], axis=1))
        blurred = dot(jnp.concatenate(parts, axis=0), df_s[v], 1)
        for p in range(planes):
            b = blurred[p * inner:(p + 1) * inner]
            recip[v, p] = jnp.where(inside, 1.0 / b, 0.0)

    sel = jnp.concatenate([mask(from_right, height)] * groups, axis=1)

    def send_edges(v):
        arrive(((has_up, to_down[1 + v]), (has_down, to_up[1 + v])))
        quot = []
        for p in range(planes):
            data = jnp.concatenate(
                [vu[v, p].astype(F32), views_v[v, p].astype(F32), vd[v, p].astype(F32)], axis=0
            )
            quot.append((data * recip[v, p]).astype(BF))
        g_v = dot(kt_s[v], jnp.concatenate(quot, axis=1))
        gbuf[v] = g_v
        for g in range(groups):
            tiles = [g_v[:, (g * per + k) * width:(g * per + k + 1) * width] for k in range(per)]
            gedge[v, :, g * width:(g + 1) * width] = pack(tiles).astype(BF)
        start(((has_left, to_left[1 + v]), (has_right, to_right[1 + v])))

    def corrected(v):
        arrive(((has_left, to_right[1 + v]), (has_right, to_left[1 + v])))
        halo = jnp.where(sel, gedge_r[v].astype(F32), gedge_l[v].astype(F32))
        parts, rest = [], []
        for p in range(planes):
            g, k = divmod(p, per)
            own = gbuf[v, :, p * width:(p + 1) * width]
            high = own.astype(BF)
            rest.append((own - high.astype(F32)).astype(BF))
            side = unpack(halo[:, g * width:(g + 1) * width], k).astype(BF)
            parts.append(jnp.concatenate([high, side], axis=1))
        corr = dot(jnp.concatenate(parts, axis=0), da_s[v])
        corr = corr + dot(jnp.concatenate(rest, axis=0), da_s[v, :width, :])
        corr = corr.reshape(planes, height, width)
        out_ref[...] = corr if v == 0 else out_ref[...] * corr

    for v in range(views):
        send_edges(v)
    for v in range(views):
        corrected(v)

    for has, copies in ((has_up, to_up), (has_down, to_down), (has_left, to_left), (has_right, to_right)):
        @pl.when(has)
        def _(copies=copies):
            for copy in copies:
                copy.wait_send()


def local_step(nr, nc, estimate, views_data, psf_rows, psf_cols):
    views, planes, height, width = views_data.shape
    taps = psf_rows.shape[1]
    reach = (taps - 1) // 2
    inner, outer = height + 2 * reach, height + 4 * reach
    per = width // (2 * reach)
    groups = planes // per
    vm = pltpu.VMEM
    any_spec = pl.BlockSpec(memory_space=pl.ANY)
    product = pl.pallas_call(
        functools.partial(kernel, nr, nc, reach),
        out_shape=jax.ShapeDtypeStruct((planes, height, width), F32),
        in_specs=[any_spec] * 4,
        out_specs=pl.BlockSpec(memory_space=pltpu.VMEM),
        scratch_shapes=[
            vm((planes, height, width), F32),
            vm((views, planes, height, width), BF),
            vm((views, planes, reach, width), BF),
            vm((views, planes, reach, width), BF),
            vm((views, taps), F32),
            vm((views, taps), F32),
            vm((2 * views, width), F32),
            vm((views * inner, outer), BF),
            vm((views, height, inner), BF),
            vm((views, width, 2 * width), BF),
            vm((views, 2 * width, width), BF),
            vm((3, height, planes * width), BF),
            vm((views * inner, planes * width), BF),
            vm((views, planes, inner, width), F32),
            vm((outer, groups * width), BF),
            vm((outer, groups * width), BF),
            vm((outer, groups * width), BF),
            vm((views, height, planes * width), F32),
            vm((views, height, groups * width), BF),
            vm((views, height, groups * width), BF),
            vm((views, height, groups * width), BF),
            pltpu.SemaphoreType.DMA((4,)),
            pltpu.SemaphoreType.DMA((4 + 4 * views,)),
            pltpu.SemaphoreType.DMA((4 + 4 * views,)),
        ],
        compiler_params=pltpu.CompilerParams(collective_id=0, has_side_effects=True),
        name="deconvolve",
    )(estimate, views_data, psf_rows, psf_cols)
    return estimate * jnp.sqrt(jnp.sqrt(product))


def solution(mesh):
    nr, nc = mesh.shape["row"], mesh.shape["col"]
    return jax.shard_map(
        functools.partial(local_step, nr, nc),
        mesh=mesh,
        in_specs=(P(None, "row", "col"), P(None, None, "row", "col"), P(), P()),
        out_specs=P(None, "row", "col"),
        check_vma=False,
    )
```

```python
import functools

import jax
import jax.numpy as jnp
from jax import lax
from jax.experimental import pallas as pl
from jax.experimental.pallas import tpu as pltpu
from jax.sharding import PartitionSpec as P

BF = jnp.bfloat16
F32 = jnp.float32
MESH = pl.DeviceIdType.MESH


def dot(a, b, contract_b=0):
    return lax.dot_general(
        a, b, (((1,), (contract_b,)), ((), ())), preferred_element_type=F32
    )


def kernel(
    nr, nc, reach,
    est_hbm, views_hbm, pr_hbm, pc_hbm, out_ref,
    est_v, views_v, pr_v, pc_v, kp, ky_s, kt_s, df_s, da_s,
    ext, ybuf, quot, edge, edge_l, edge_r, gbuf, gedge, gedge_l, gedge_r,
    local_sem, send_sem, recv_sem,
):
    views, planes, height, width = views_v.shape
    taps = pr_v.shape[1]
    inner = height + 2 * reach
    per = width // (2 * reach)
    groups = planes // per
    r, c = lax.axis_index("row"), lax.axis_index("col")
    up, down = (r - 1, c), (r + 1, c)
    left, right = (r, c - 1), (r, c + 1)
    has_up, has_down, has_left, has_right = r > 0, r < nr - 1, c > 0, c < nc - 1
    corners = (
        (has_up & has_left, (r - 1, c - 1)), (has_up & has_right, (r - 1, c + 1)),
        (has_down & has_left, (r + 1, c - 1)), (has_down & has_right, (r + 1, c + 1)),
    )
    sides = ((has_up, up), (has_down, down), (has_left, left), (has_right, right)) + corners

    local = [
        pltpu.make_async_copy(s, d, local_sem.at[i])
        for i, (s, d) in enumerate(
            ((est_hbm, est_v), (pr_hbm, pr_v), (pc_hbm, pc_v), (views_hbm, views_v))
        )
    ]
    for copy in local:
        copy.start()

    barrier = pltpu.get_barrier_semaphore()
    for has, where in sides:
        @pl.when(has)
        def _():
            pl.semaphore_signal(barrier, inc=1, device_id=where, device_id_type=MESH)

    def remote(src, dst, slot, where):
        return pltpu.make_async_remote_copy(
            src_ref=src, dst_ref=dst, send_sem=send_sem.at[slot],
            recv_sem=recv_sem.at[slot], device_id=where, device_id_type=MESH,
        )

    first, last = pl.ds(reach, reach), pl.ds(height, reach)
    above, middle, below = pl.ds(0, reach), pl.ds(reach, height), pl.ds(reach + height, reach)
    quot_at, gedge_at = 8, 8 + 2 * views
    to_up = [remote(ext.at[first], ext.at[below], 0, up)] + [
        remote(quot.at[v, first], quot.at[v, below], quot_at + v, up) for v in range(views)
    ]
    to_down = [remote(ext.at[last], ext.at[above], 1, down)] + [
        remote(quot.at[v, last], quot.at[v, above], quot_at + views + v, down) for v in range(views)
    ]
    to_left = [remote(edge.at[middle], edge_r.at[middle], 2, left)] + [
        remote(gedge.at[v], gedge_r.at[v], gedge_at + v, left) for v in range(views)
    ]
    to_right = [remote(edge.at[middle], edge_l.at[middle], 3, right)] + [
        remote(gedge.at[v], gedge_l.at[v], gedge_at + views + v, right) for v in range(views)
    ]
    to_corner = [
        remote(edge.at[first], edge_r.at[below], 4, corners[0][1]),
        remote(edge.at[first], edge_l.at[below], 5, corners[1][1]),
        remote(edge.at[last], edge_r.at[above], 6, corners[2][1]),
        remote(edge.at[last], edge_l.at[above], 7, corners[3][1]),
    ]

    def start(which):
        for has, copies in which:
            @pl.when(has)
            def _(copies=copies):
                copies.start()

    def arrive(which):
        for has, copies in which:
            @pl.when(has)
            def _(copies=copies):
                copies.wait_recv()

    lane = lax.broadcasted_iota(jnp.int32, (8, width), 1)
    slot_of = ((lane + reach) // (2 * reach)) % per
    from_right = (lane // reach) % 2 == 0

    def mask(m, rows):
        return jnp.broadcast_to(m[:1], (rows, width))

    def pack(tiles):
        rows = tiles[0].shape[0]
        total = tiles[0]
        for k in range(1, per):
            total = jnp.where(mask(slot_of, rows) == k, pltpu.roll(tiles[k], 2 * reach * k, 1), total)
        return total.astype(BF)

    def unpack(tile, k):
        return tile if k == 0 else pltpu.roll(tile, width - 2 * reach * k, 1)

    local[0].wait()
    for p in range(planes):
        ext[middle, p * width:(p + 1) * width] = est_v[p].astype(BF)
    for g in range(groups):
        edge[middle, g * width:(g + 1) * width] = pack([est_v[g * per + k] for k in range(per)])
    peers = 0
    for has, where in sides:
        peers = peers + has.astype(jnp.int32)
    pl.semaphore_wait(barrier, peers)
    start(((has_up, to_up[0]), (has_down, to_down[0])))
    start([(has, copy) for (has, _), copy in zip(corners, to_corner)])
    start(((has_left, to_left[0]), (has_right, to_right[0])))

    def clear(has, refs):
        @pl.when(jnp.logical_not(has))
        def _():
            for ref in refs:
                ref[...] = jnp.zeros(ref.shape, ref.dtype)

    clear(has_up, [ext.at[above]] + [quot.at[v, above] for v in range(views)])
    clear(has_down, [ext.at[below]] + [quot.at[v, below] for v in range(views)])
    clear(has_left, [edge_l.at[middle], gedge_l])
    clear(has_right, [edge_r.at[middle], gedge_r])
    for (has, _), ref in zip(
        corners, (edge_l.at[above], edge_r.at[above], edge_l.at[below], edge_r.at[below])
    ):
        clear(has, [ref])

    local[1].wait()
    local[2].wait()
    kp[...] = jnp.zeros(kp.shape, F32)
    psf_y, psf_x = pr_v[...], pc_v[...]
    kp[0:views, 0:taps] = psf_y / jnp.sum(psf_y, axis=1, keepdims=True)
    kp[views:2 * views, 0:taps] = psf_x / jnp.sum(psf_x, axis=1, keepdims=True)
    square = (width, width)
    apart = lax.broadcasted_iota(jnp.int32, square, 1) - lax.broadcasted_iota(jnp.int32, square, 0)
    near = (apart <= reach) & (apart >= -reach)
    for v in range(views):
        rows_y = jnp.broadcast_to(kp[v:v + 1, :], square)
        by = pltpu.roll(rows_y, 0, 1, stride=1, stride_axis=0)
        ky_s[v * height:(v + 1) * height, :] = by[:height, :inner].astype(BF)
        kt_s[v] = by.T[2 * reach:2 * reach + height, :inner].astype(BF)
        rows_x = jnp.broadcast_to(kp[views + v:views + v + 1, :], square)
        bx = pltpu.roll(rows_x, width - reach, 1, stride=1, stride_axis=0)
        core = jnp.where(near, bx, 0.0).astype(BF)
        off = jnp.where(near, 0.0, bx).astype(BF)
        df_s[v, :, :width] = core
        df_s[v, :, width:] = off
        da_s[v, :width, :] = core
        da_s[v, width:, :] = off

    arrive(((has_up, to_down[0]), (has_down, to_up[0])))
    ybuf[...] = dot(ky_s[...], ext[...]).astype(BF)
    arrive(((has_left, to_right[0]), (has_right, to_left[0])))
    arrive([(has, copy) for (has, _), copy in zip(corners, reversed(to_corner))])
    sel = jnp.concatenate([mask(from_right, inner)] * groups, axis=1)
    edges = jnp.where(sel, edge_r[...].astype(F32), edge_l[...].astype(F32)).astype(BF)
    y_edges = dot(ky_s[...], edges)

    local[3].wait()
    for v in range(views):
        vs = slice(v * height, (v + 1) * height)
        parts = []
        for p in range(planes):
            g, k = divmod(p, per)
            halo = unpack(y_edges[vs, g * width:(g + 1) * width], k).astype(BF)
            parts.append(jnp.concatenate([ybuf[vs, p * width:(p + 1) * width], halo], axis=1))
        blurred = dot(jnp.concatenate(parts, axis=0), df_s[v], 1)
        for p in range(planes):
            ratio = views_v[v, p].astype(F32) / blurred[p * height:(p + 1) * height]
            quot[v, middle, p * width:(p + 1) * width] = ratio.astype(BF)
        start(((has_up, to_up[1 + v]), (has_down, to_down[1 + v])))

    for v in range(views):
        arrive(((has_up, to_down[1 + v]), (has_down, to_up[1 + v])))
        g_v = dot(kt_s[v], quot[v])
        gbuf[v] = g_v
        for g in range(groups):
            tiles = [g_v[:, (g * per + k) * width:(g * per + k + 1) * width] for k in range(per)]
            gedge[v, :, g * width:(g + 1) * width] = pack(tiles)
        start(((has_left, to_left[1 + v]), (has_right, to_right[1 + v])))

    sel = jnp.concatenate([mask(from_right, height)] * groups, axis=1)
    product = None
    for v in range(views):
        arrive(((has_left, to_right[1 + v]), (has_right, to_left[1 + v])))
        halo = jnp.where(sel, gedge_r[v].astype(F32), gedge_l[v].astype(F32))
        parts, rest = [], []
        for p in range(planes):
            g, k = divmod(p, per)
            own = gbuf[v, :, p * width:(p + 1) * width]
            high = own.astype(BF)
            rest.append((own - high.astype(F32)).astype(BF))
            side = unpack(halo[:, g * width:(g + 1) * width], k).astype(BF)
            parts.append(jnp.concatenate([high, side], axis=1))
        corr = dot(jnp.concatenate(parts, axis=0), da_s[v])
        corr = corr + dot(jnp.concatenate(rest, axis=0), da_s[v, :width, :])
        product = corr if product is None else product * corr
    out_ref[...] = est_v[...] * jnp.sqrt(jnp.sqrt(product)).reshape(planes, height, width)

    ends = ((has_up, to_up), (has_down, to_down), (has_left, to_left), (has_right, to_right))
    for has, copies in ends + tuple((has, [copy]) for (has, _), copy in zip(corners, to_corner)):
        @pl.when(has)
        def _(copies=copies):
            for copy in copies:
                copy.wait_send()


def local_step(nr, nc, estimate, views_data, psf_rows, psf_cols):
    views, planes, height, width = views_data.shape
    taps = psf_rows.shape[1]
    reach = (taps - 1) // 2
    inner = height + 2 * reach
    per = width // (2 * reach)
    groups = planes // per
    vm = pltpu.VMEM
    any_spec = pl.BlockSpec(memory_space=pl.ANY)
    return pl.pallas_call(
        functools.partial(kernel, nr, nc, reach),
        out_shape=jax.ShapeDtypeStruct((planes, height, width), F32),
        in_specs=[any_spec] * 4,
        out_specs=pl.BlockSpec(memory_space=pltpu.VMEM),
        scratch_shapes=[
            vm((planes, height, width), F32),
            vm((views, planes, height, width), BF),
            vm((views, taps), F32),
            vm((views, taps), F32),
            vm((2 * views, width), F32),
            vm((views * height, inner), BF),
            vm((views, height, inner), BF),
            vm((views, width, 2 * width), BF),
            vm((views, 2 * width, width), BF),
            vm((inner, planes * width), BF),
            vm((views * height, planes * width), BF),
            vm((views, inner, planes * width), BF),
            vm((inner, groups * width), BF),
            vm((inner, groups * width), BF),
            vm((inner, groups * width), BF),
            vm((views, height, planes * width), F32),
            vm((views, height, groups * width), BF),
            vm((views, height, groups * width), BF),
            vm((views, height, groups * width), BF),
            pltpu.SemaphoreType.DMA((4,)),
            pltpu.SemaphoreType.DMA((8 + 4 * views,)),
            pltpu.SemaphoreType.DMA((8 + 4 * views,)),
        ],
        compiler_params=pltpu.CompilerParams(collective_id=0, has_side_effects=True),
        name="deconvolve",
    )(estimate, views_data, psf_rows, psf_cols)


def solution(mesh):
    nr, nc = mesh.shape["row"], mesh.shape["col"]
    return jax.shard_map(
        functools.partial(local_step, nr, nc),
        mesh=mesh,
        in_specs=(P(None, "row", "col"), P(None, None, "row", "col"), P(), P()),
        out_specs=P(None, "row", "col"),
        check_vma=False,
    )
```

```python
import functools

import jax
import jax.numpy as jnp
from jax import lax
from jax.experimental import pallas as pl
from jax.experimental.pallas import tpu as pltpu
from jax.sharding import PartitionSpec as P

BF = jnp.bfloat16
F32 = jnp.float32
MESH = pl.DeviceIdType.MESH


def dot(a, b, contract_b=0):
    return lax.dot_general(
        a, b, (((1,), (contract_b,)), ((), ())), preferred_element_type=F32
    )


def kernel(
    nr, nc, reach,
    est_hbm, views_hbm, psf, out_ref,
    est_v, views_v, ky_s, kt_s, df_s, da_s,
    ext, ybuf, quot, edge, edge_l, edge_r, gbuf, gedge, gedge_l, gedge_r,
    local_sem, send_sem, recv_sem,
):
    views, planes, height, width = views_v.shape
    inner = height + 2 * reach
    per = width // (2 * reach)
    groups = planes // per
    r, c = lax.axis_index("row"), lax.axis_index("col")
    up, down = (r - 1, c), (r + 1, c)
    left, right = (r, c - 1), (r, c + 1)
    has_up, has_down, has_left, has_right = r > 0, r < nr - 1, c > 0, c < nc - 1
    corners = (
        (has_up & has_left, (r - 1, c - 1)), (has_up & has_right, (r - 1, c + 1)),
        (has_down & has_left, (r + 1, c - 1)), (has_down & has_right, (r + 1, c + 1)),
    )
    sides = ((has_up, up), (has_down, down), (has_left, left), (has_right, right)) + corners

    local = [
        pltpu.make_async_copy(s, d, local_sem.at[i])
        for i, (s, d) in enumerate(((est_hbm, est_v), (views_hbm, views_v)))
    ]
    for copy in local:
        copy.start()

    barrier = pltpu.get_barrier_semaphore()
    for has, where in sides:
        @pl.when(has)
        def _():
            pl.semaphore_signal(barrier, inc=1, device_id=where, device_id_type=MESH)

    def remote(src, dst, slot, where):
        return pltpu.make_async_remote_copy(
            src_ref=src, dst_ref=dst, send_sem=send_sem.at[slot],
            recv_sem=recv_sem.at[slot], device_id=where, device_id_type=MESH,
        )

    first, last = pl.ds(reach, reach), pl.ds(height, reach)
    above, middle, below = pl.ds(0, reach), pl.ds(reach, height), pl.ds(reach + height, reach)
    quot_at, gedge_at = 8, 8 + 2 * views
    to_up = [remote(ext.at[first], ext.at[below], 0, up)] + [
        remote(quot.at[v, first], quot.at[v, below], quot_at + v, up) for v in range(views)
    ]
    to_down = [remote(ext.at[last], ext.at[above], 1, down)] + [
        remote(quot.at[v, last], quot.at[v, above], quot_at + views + v, down) for v in range(views)
    ]
    to_left = [remote(edge.at[middle], edge_r.at[middle], 2, left)] + [
        remote(gedge.at[v], gedge_r.at[v], gedge_at + v, left) for v in range(views)
    ]
    to_right = [remote(edge.at[middle], edge_l.at[middle], 3, right)] + [
        remote(gedge.at[v], gedge_l.at[v], gedge_at + views + v, right) for v in range(views)
    ]
    to_corner = [
        remote(edge.at[first], edge_r.at[below], 4, corners[0][1]),
        remote(edge.at[first], edge_l.at[below], 5, corners[1][1]),
        remote(edge.at[last], edge_r.at[above], 6, corners[2][1]),
        remote(edge.at[last], edge_l.at[above], 7, corners[3][1]),
    ]

    def start(which):
        for has, copies in which:
            @pl.when(has)
            def _(copies=copies):
                copies.start()

    def arrive(which):
        for has, copies in which:
            @pl.when(has)
            def _(copies=copies):
                copies.wait_recv()

    lane = lax.broadcasted_iota(jnp.int32, (8, width), 1)
    slot_of = ((lane + reach) // (2 * reach)) % per
    from_right = (lane // reach) % 2 == 0

    def mask(m, rows):
        return jnp.broadcast_to(m[:1], (rows, width))

    def pack(tiles):
        rows = tiles[0].shape[0]
        total = tiles[0]
        for k in range(1, per):
            total = jnp.where(mask(slot_of, rows) == k, pltpu.roll(tiles[k], 2 * reach * k, 1), total)
        return total.astype(BF)

    def unpack(tile, k):
        return tile if k == 0 else pltpu.roll(tile, width - 2 * reach * k, 1)

    local[0].wait()
    for p in range(planes):
        ext[middle, p * width:(p + 1) * width] = est_v[p].astype(BF)
    for g in range(groups):
        edge[middle, g * width:(g + 1) * width] = pack([est_v[g * per + k] for k in range(per)])
    peers = 0
    for has, where in sides:
        peers = peers + has.astype(jnp.int32)
    pl.semaphore_wait(barrier, peers)
    start(((has_up, to_up[0]), (has_down, to_down[0])))
    start([(has, copy) for (has, _), copy in zip(corners, to_corner)])
    start(((has_left, to_left[0]), (has_right, to_right[0])))

    def clear(has, refs):
        @pl.when(jnp.logical_not(has))
        def _():
            for ref in refs:
                ref[...] = jnp.zeros(ref.shape, ref.dtype)

    clear(has_up, [ext.at[above]] + [quot.at[v, above] for v in range(views)])
    clear(has_down, [ext.at[below]] + [quot.at[v, below] for v in range(views)])
    clear(has_left, [edge_l.at[middle], gedge_l])
    clear(has_right, [edge_r.at[middle], gedge_r])
    for (has, _), ref in zip(
        corners, (edge_l.at[above], edge_r.at[above], edge_l.at[below], edge_r.at[below])
    ):
        clear(has, [ref])

    taps = psf[...] / jnp.sum(psf[...], axis=1, keepdims=True)
    square = (width, width)
    apart = lax.broadcasted_iota(jnp.int32, square, 1) - lax.broadcasted_iota(jnp.int32, square, 0)
    near = (apart <= reach) & (apart >= -reach)
    for v in range(views):
        rows_y = jnp.broadcast_to(taps[v:v + 1], square)
        by = pltpu.roll(rows_y, 0, 1, stride=1, stride_axis=0)
        ky_s[v * height:(v + 1) * height, :] = by[:height, :inner].astype(BF)
        kt_s[v] = by.T[2 * reach:2 * reach + height, :inner].astype(BF)
        rows_x = jnp.broadcast_to(taps[views + v:views + v + 1], square)
        bx = pltpu.roll(rows_x, width - reach, 1, stride=1, stride_axis=0)
        core = jnp.where(near, bx, 0.0).astype(BF)
        off = jnp.where(near, 0.0, bx).astype(BF)
        df_s[v, :, :width] = core
        df_s[v, :, width:] = off
        da_s[v, :width, :] = core
        da_s[v, width:, :] = off

    arrive(((has_up, to_down[0]), (has_down, to_up[0])))
    ybuf[...] = dot(ky_s[...], ext[...]).astype(BF)
    arrive(((has_left, to_right[0]), (has_right, to_left[0])))
    arrive([(has, copy) for (has, _), copy in zip(corners, reversed(to_corner))])
    sel = jnp.concatenate([mask(from_right, inner)] * groups, axis=1)
    edges = jnp.where(sel, edge_r[...].astype(F32), edge_l[...].astype(F32)).astype(BF)
    y_edges = dot(ky_s[...], edges)

    local[1].wait()
    for v in range(views):
        vs = slice(v * height, (v + 1) * height)
        parts = []
        for p in range(planes):
            g, k = divmod(p, per)
            halo = unpack(y_edges[vs, g * width:(g + 1) * width], k).astype(BF)
            parts.append(jnp.concatenate([ybuf[vs, p * width:(p + 1) * width], halo], axis=1))
        blurred = dot(jnp.concatenate(parts, axis=0), df_s[v], 1)
        for p in range(planes):
            ratio = views_v[v, p].astype(F32) / blurred[p * height:(p + 1) * height]
            quot[v, middle, p * width:(p + 1) * width] = ratio.astype(BF)
        start(((has_up, to_up[1 + v]), (has_down, to_down[1 + v])))

    for v in range(views):
        arrive(((has_up, to_down[1 + v]), (has_down, to_up[1 + v])))
        g_v = dot(kt_s[v], quot[v])
        gbuf[v] = g_v
        for g in range(groups):
            tiles = [g_v[:, (g * per + k) * width:(g * per + k + 1) * width] for k in range(per)]
            gedge[v, :, g * width:(g + 1) * width] = pack(tiles)
        start(((has_left, to_left[1 + v]), (has_right, to_right[1 + v])))

    sel = jnp.concatenate([mask(from_right, height)] * groups, axis=1)
    product = None
    for v in range(views):
        arrive(((has_left, to_right[1 + v]), (has_right, to_left[1 + v])))
        halo = jnp.where(sel, gedge_r[v].astype(F32), gedge_l[v].astype(F32))
        parts, rest = [], []
        for p in range(planes):
            g, k = divmod(p, per)
            own = gbuf[v, :, p * width:(p + 1) * width]
            high = own.astype(BF)
            rest.append((own - high.astype(F32)).astype(BF))
            side = unpack(halo[:, g * width:(g + 1) * width], k).astype(BF)
            parts.append(jnp.concatenate([high, side], axis=1))
        corr = dot(jnp.concatenate(parts, axis=0), da_s[v])
        corr = corr + dot(jnp.concatenate(rest, axis=0), da_s[v, :width, :])
        product = corr if product is None else product * corr
    out_ref[...] = est_v[...] * jnp.sqrt(jnp.sqrt(product)).reshape(planes, height, width)

    ends = ((has_up, to_up), (has_down, to_down), (has_left, to_left), (has_right, to_right))
    for has, copies in ends + tuple((has, [copy]) for (has, _), copy in zip(corners, to_corner)):
        @pl.when(has)
        def _(copies=copies):
            for copy in copies:
                copy.wait_send()


def local_step(nr, nc, estimate, views_data, psf_rows, psf_cols):
    views, planes, height, width = views_data.shape
    taps = psf_rows.shape[1]
    reach = (taps - 1) // 2
    inner = height + 2 * reach
    per = width // (2 * reach)
    groups = planes // per
    psf = jnp.concatenate([psf_rows, psf_cols])
    psf = jnp.pad(psf, ((0, 0), (0, width - taps)))
    vm = pltpu.VMEM
    any_spec = pl.BlockSpec(memory_space=pl.ANY)
    return pl.pallas_call(
        functools.partial(kernel, nr, nc, reach),
        out_shape=jax.ShapeDtypeStruct((planes, height, width), F32),
        in_specs=[any_spec] * 2 + [pl.BlockSpec(memory_space=pltpu.VMEM)],
        out_specs=pl.BlockSpec(memory_space=pltpu.VMEM),
        scratch_shapes=[
            vm((planes, height, width), F32),
            vm((views, planes, height, width), BF),
            vm((views * height, inner), BF),
            vm((views, height, inner), BF),
            vm((views, width, 2 * width), BF),
            vm((views, 2 * width, width), BF),
            vm((inner, planes * width), BF),
            vm((views * height, planes * width), BF),
            vm((views, inner, planes * width), BF),
            vm((inner, groups * width), BF),
            vm((inner, groups * width), BF),
            vm((inner, groups * width), BF),
            vm((views, height, planes * width), F32),
            vm((views, height, groups * width), BF),
            vm((views, height, groups * width), BF),
            vm((views, height, groups * width), BF),
            pltpu.SemaphoreType.DMA((2,)),
            pltpu.SemaphoreType.DMA((8 + 4 * views,)),
            pltpu.SemaphoreType.DMA((8 + 4 * views,)),
        ],
        compiler_params=pltpu.CompilerParams(
            collective_id=0, has_side_effects=True, vmem_limit_bytes=55036 * 1024
        ),
        name="deconvolve",
    )(estimate, views_data, psf)


def solution(mesh):
    nr, nc = mesh.shape["row"], mesh.shape["col"]
    return jax.shard_map(
        functools.partial(local_step, nr, nc),
        mesh=mesh,
        in_specs=(P(None, "row", "col"), P(None, None, "row", "col"), P(), P()),
        out_specs=P(None, "row", "col"),
        check_vma=False,
    )
```

```python
import functools

import jax
import jax.numpy as jnp
from jax import lax
from jax.experimental import pallas as pl
from jax.experimental.pallas import tpu as pltpu
from jax.sharding import PartitionSpec as P

BF = jnp.bfloat16
F32 = jnp.float32
MESH = pl.DeviceIdType.MESH


def dot(a, b, contract_b=0):
    return lax.dot_general(
        a, b, (((1,), (contract_b,)), ((), ())), preferred_element_type=F32
    )


def kernel(
    nr, nc, reach,
    est_hbm, views_hbm, psf, out_ref,
    est_v, views_v, ky_s, kt_s, df_s, da_s,
    ext, ybuf, quot, edge, side, qedge, qside,
    local_sem, send_sem, recv_sem,
):
    views, planes, height, width = views_v.shape
    inner = height + 2 * reach
    r, c = lax.axis_index("row"), lax.axis_index("col")
    up, down = (r - 1, c), (r + 1, c)
    left, right = (r, c - 1), (r, c + 1)
    has_up, has_down, has_left, has_right = r > 0, r < nr - 1, c > 0, c < nc - 1
    corners = (
        (has_up & has_left, (r - 1, c - 1)), (has_up & has_right, (r - 1, c + 1)),
        (has_down & has_left, (r + 1, c - 1)), (has_down & has_right, (r + 1, c + 1)),
    )
    sides = ((has_up, up), (has_down, down), (has_left, left), (has_right, right)) + corners

    local = [
        pltpu.make_async_copy(s, d, local_sem.at[i])
        for i, (s, d) in enumerate(((est_hbm, est_v), (views_hbm, views_v)))
    ]
    for copy in local:
        copy.start()

    barrier = pltpu.get_barrier_semaphore()
    for has, where in sides:
        @pl.when(has)
        def _():
            pl.semaphore_signal(barrier, inc=1, device_id=where, device_id_type=MESH)

    def remote(src, dst, slot, where):
        return pltpu.make_async_remote_copy(
            src_ref=src, dst_ref=dst, send_sem=send_sem.at[slot],
            recv_sem=recv_sem.at[slot], device_id=where, device_id_type=MESH,
        )

    first, last = pl.ds(reach, reach), pl.ds(height, reach)
    above, middle, below = pl.ds(0, reach), pl.ds(reach, height), pl.ds(reach + height, reach)
    quot_at, edge_at, pairs = 8, 8 + 2 * views, views // 2
    to_up = [remote(ext.at[first], ext.at[below], 0, up)] + [
        remote(quot.at[v, first], quot.at[v, below], quot_at + v, up) for v in range(views)
    ]
    to_down = [remote(ext.at[last], ext.at[above], 1, down)] + [
        remote(quot.at[v, last], quot.at[v, above], quot_at + views + v, down) for v in range(views)
    ]
    ways = (
        (0, middle, middle, has_left, left), (1, middle, middle, has_right, right),
        (0, first, below) + corners[0], (1, first, below) + corners[1],
        (0, last, above) + corners[2], (1, last, above) + corners[3],
    )
    opposite = (1, 0, 5, 4, 3, 2)
    est_ways = [
        (has, remote(edge.at[s, src], side.at[s, dst], 2 + i, where))
        for i, (s, src, dst, has, where) in enumerate(ways)
    ]
    quot_ways = [
        [
            (has, remote(
                qedge.at[s, pl.ds(2 * k, 2), src], qside.at[s, pl.ds(2 * k, 2), dst],
                edge_at + 6 * k + i, where,
            ))
            for i, (s, src, dst, has, where) in enumerate(ways)
        ]
        for k in range(pairs)
    ]

    def start(which):
        for has, copies in which:
            @pl.when(has)
            def _(copies=copies):
                copies.start()

    def arrive_edges(sent):
        arrive([(ways[j][3], sent[i][1]) for i, j in enumerate(opposite)])

    def arrive(which):
        for has, copies in which:
            @pl.when(has)
            def _(copies=copies):
                copies.wait_recv()

    lane = lax.broadcasted_iota(jnp.int32, (8, width), 1)
    group = lane // reach
    near_right = lane < width // 2

    def mask(m, rows):
        return jnp.broadcast_to(m[:1], (rows, width))

    def pack(tiles):
        rows = tiles[0].shape[0]
        turned = [t if k == 0 else pltpu.roll(t, reach * k, 1) for k, t in enumerate(tiles)]
        here, there = turned[0], turned[0]
        for k in range(1, planes):
            here = jnp.where(mask(group, rows) == k, turned[k], here)
            there = jnp.where(mask(group, rows) == k - 1, turned[k], there)
        return here.astype(BF), there.astype(BF)

    def unpack(edges, k):
        rows = edges.shape[0]
        tiles = (edges[:, :width], edges[:, width:])
        if k:
            tiles = [pltpu.roll(t, width - reach * k, 1) for t in tiles]
        return jnp.where(mask(near_right, rows), tiles[0], tiles[1]).astype(BF)

    local[0].wait()
    for p in range(planes):
        ext[middle, p * width:(p + 1) * width] = est_v[p].astype(BF)
    here, there = pack([est_v[p] for p in range(planes)])
    edge[0, middle], edge[1, middle] = here, there
    peers = 0
    for has, where in sides:
        peers = peers + has.astype(jnp.int32)
    pl.semaphore_wait(barrier, peers)
    start(((has_up, to_up[0]), (has_down, to_down[0])))
    start(est_ways)

    def clear(has, refs):
        @pl.when(jnp.logical_not(has))
        def _():
            for ref in refs:
                ref[...] = jnp.zeros(ref.shape, ref.dtype)

    clear(has_up, [ext.at[above]] + [quot.at[v, above] for v in range(views)])
    clear(has_down, [ext.at[below]] + [quot.at[v, below] for v in range(views)])
    for i, j in enumerate(opposite):
        s, _, dst, _, _ = ways[i]
        clear(ways[j][3], [side.at[s, dst]] + [qside.at[s, v, dst] for v in range(views)])

    taps = psf[...] / jnp.sum(psf[...], axis=1, keepdims=True)
    square = (width, width)
    apart = lax.broadcasted_iota(jnp.int32, square, 1) - lax.broadcasted_iota(jnp.int32, square, 0)
    near = (apart <= reach) & (apart >= -reach)
    for v in range(views):
        rows_y = jnp.broadcast_to(taps[v:v + 1], square)
        by = pltpu.roll(rows_y, 0, 1, stride=1, stride_axis=0)
        ky_s[v * height:(v + 1) * height, :] = by[:height, :inner].astype(BF)
        kt_s[v] = by.T[2 * reach:2 * reach + height, :inner].astype(BF)
        rows_x = jnp.broadcast_to(taps[views + v:views + v + 1], square)
        bx = pltpu.roll(rows_x, width - reach, 1, stride=1, stride_axis=0)
        core = jnp.where(near, bx, 0.0).astype(BF)
        off = jnp.where(near, 0.0, bx).astype(BF)
        df_s[v, :, :width] = core
        df_s[v, :, width:] = off
        da_s[v, :width, :] = core
        da_s[v, width:, :] = off

    arrive(((has_up, to_down[0]), (has_down, to_up[0])))
    ybuf[...] = dot(ky_s[...], ext[...]).astype(BF)
    arrive_edges(est_ways)
    y_edges = dot(ky_s[...], jnp.concatenate([side[0], side[1]], axis=1))

    local[1].wait()
    for v in range(views):
        vs = slice(v * height, (v + 1) * height)
        parts = []
        for p in range(planes):
            halo = unpack(y_edges[vs], p)
            parts.append(jnp.concatenate([ybuf[vs, p * width:(p + 1) * width], halo], axis=1))
        blurred = dot(jnp.concatenate(parts, axis=0), df_s[v], 1)
        ratios = [
            views_v[v, p].astype(F32) / blurred[p * height:(p + 1) * height] for p in range(planes)
        ]
        for p in range(planes):
            quot[v, middle, p * width:(p + 1) * width] = ratios[p].astype(BF)
        if v % 2 == 0:
            start(((has_up, to_up[1 + v]), (has_down, to_down[1 + v])))
        qedge[0, v, middle], qedge[1, v, middle] = pack(ratios)
        if v % 2 == 1:
            start(quot_ways[v // 2])
            start(((has_up, to_up[1 + v]), (has_down, to_down[1 + v])))

    product = None
    for v in range(views):
        arrive(((has_up, to_down[1 + v]), (has_down, to_up[1 + v])))
        g_own = dot(kt_s[v], quot[v])
        if v % 2 == 0:
            arrive_edges(quot_ways[v // 2])
        g_edges = dot(kt_s[v], jnp.concatenate([qside[0, v], qside[1, v]], axis=1))
        parts, rest = [], []
        for p in range(planes):
            own = g_own[:, p * width:(p + 1) * width]
            high = own.astype(BF)
            rest.append((own - high.astype(F32)).astype(BF))
            parts.append(jnp.concatenate([high, unpack(g_edges, p)], axis=1))
        corr = dot(jnp.concatenate(parts, axis=0), da_s[v])
        corr = corr + dot(jnp.concatenate(rest, axis=0), da_s[v, :width, :])
        product = corr if product is None else product * corr
    out_ref[...] = est_v[...] * jnp.sqrt(jnp.sqrt(product)).reshape(planes, height, width)

    sent = [(has_up, to_up), (has_down, to_down)]
    sent += [(has, [copy]) for some in [est_ways] + quot_ways for has, copy in some]
    for has, copies in sent:
        @pl.when(has)
        def _(copies=copies):
            for copy in copies:
                copy.wait_send()


def local_step(nr, nc, estimate, views_data, psf_rows, psf_cols):
    views, planes, height, width = views_data.shape
    taps = psf_rows.shape[1]
    reach = (taps - 1) // 2
    inner = height + 2 * reach
    psf = jnp.concatenate([psf_rows, psf_cols])
    psf = jnp.pad(psf, ((0, 0), (0, width - taps)))
    vm = pltpu.VMEM
    any_spec = pl.BlockSpec(memory_space=pl.ANY)
    return pl.pallas_call(
        functools.partial(kernel, nr, nc, reach),
        out_shape=jax.ShapeDtypeStruct((planes, height, width), F32),
        in_specs=[any_spec] * 2 + [pl.BlockSpec(memory_space=pltpu.VMEM)],
        out_specs=pl.BlockSpec(memory_space=pltpu.VMEM),
        scratch_shapes=[
            vm((planes, height, width), F32),
            vm((views, planes, height, width), BF),
            vm((views * height, inner), BF),
            vm((views, height, inner), BF),
            vm((views, width, 2 * width), BF),
            vm((views, 2 * width, width), BF),
            vm((inner, planes * width), BF),
            vm((views * height, planes * width), BF),
            vm((views, inner, planes * width), BF),
            vm((2, inner, width), BF),
            vm((2, inner, width), BF),
            vm((2, views, inner, width), BF),
            vm((2, views, inner, width), BF),
            pltpu.SemaphoreType.DMA((2,)),
            pltpu.SemaphoreType.DMA((8 + 5 * views,)),
            pltpu.SemaphoreType.DMA((8 + 5 * views,)),
        ],
        compiler_params=pltpu.CompilerParams(
            collective_id=0, has_side_effects=True, vmem_limit_bytes=55036 * 1024
        ),
        name="deconvolve",
    )(estimate, views_data, psf)


def solution(mesh):
    nr, nc = mesh.shape["row"], mesh.shape["col"]
    return jax.shard_map(
        functools.partial(local_step, nr, nc),
        mesh=mesh,
        in_specs=(P(None, "row", "col"), P(None, None, "row", "col"), P(), P()),
        out_specs=P(None, "row", "col"),
        check_vma=False,
    )
```

```python
import functools

import jax
import jax.numpy as jnp
from jax import lax
from jax.experimental import pallas as pl
from jax.experimental.pallas import tpu as pltpu
from jax.sharding import PartitionSpec as P

BF = jnp.bfloat16
F32 = jnp.float32
MESH = pl.DeviceIdType.MESH


def dot(a, b, contract_b=0):
    return lax.dot_general(
        a, b, (((1,), (contract_b,)), ((), ())), preferred_element_type=F32
    )


def kernel(
    nr, nc, reach,
    est_hbm, views_hbm, psf, out_ref,
    est_v, views_v, ky_s, kt_s, df_s, da_s,
    ext, ybuf, quot, edge, side, qedge, qside,
    local_sem, send_sem, recv_sem,
):
    views, planes, height, width = views_v.shape
    inner = height + 2 * reach
    r, c = lax.axis_index("row"), lax.axis_index("col")
    up, down = (r - 1, c), (r + 1, c)
    left, right = (r, c - 1), (r, c + 1)
    has_up, has_down, has_left, has_right = r > 0, r < nr - 1, c > 0, c < nc - 1
    corners = (
        (has_up & has_left, (r - 1, c - 1)), (has_up & has_right, (r - 1, c + 1)),
        (has_down & has_left, (r + 1, c - 1)), (has_down & has_right, (r + 1, c + 1)),
    )
    sides = ((has_up, up), (has_down, down), (has_left, left), (has_right, right)) + corners

    local = [
        pltpu.make_async_copy(s, d, local_sem.at[i])
        for i, (s, d) in enumerate(((est_hbm, est_v), (views_hbm, views_v)))
    ]
    for copy in local:
        copy.start()

    barrier = pltpu.get_barrier_semaphore()
    for has, where in sides:
        @pl.when(has)
        def _():
            pl.semaphore_signal(barrier, inc=1, device_id=where, device_id_type=MESH)

    def remote(src, dst, slot, where):
        return pltpu.make_async_remote_copy(
            src_ref=src, dst_ref=dst, send_sem=send_sem.at[slot],
            recv_sem=recv_sem.at[slot], device_id=where, device_id_type=MESH,
        )

    first, last = pl.ds(reach, reach), pl.ds(height, reach)
    above, middle, below = pl.ds(0, reach), pl.ds(reach, height), pl.ds(reach + height, reach)
    quot_at, edge_at, pairs = 8, 8 + 2 * views, views // 2
    to_up = [remote(ext.at[first], ext.at[below], 0, up)] + [
        remote(quot.at[v, first], quot.at[v, below], quot_at + v, up) for v in range(views)
    ]
    to_down = [remote(ext.at[last], ext.at[above], 1, down)] + [
        remote(quot.at[v, last], quot.at[v, above], quot_at + views + v, down) for v in range(views)
    ]
    ways = (
        (0, middle, middle, has_left, left), (1, middle, middle, has_right, right),
        (0, first, below) + corners[0], (1, first, below) + corners[1],
        (0, last, above) + corners[2], (1, last, above) + corners[3],
    )
    opposite = (1, 0, 5, 4, 3, 2)
    est_ways = [
        (has, remote(edge.at[s, src], side.at[s, dst], 2 + i, where))
        for i, (s, src, dst, has, where) in enumerate(ways)
    ]
    quot_ways = [
        [
            (has, remote(
                qedge.at[s, pl.ds(2 * k, 2), src], qside.at[s, pl.ds(2 * k, 2), dst],
                edge_at + 6 * k + i, where,
            ))
            for i, (s, src, dst, has, where) in enumerate(ways)
        ]
        for k in range(pairs)
    ]

    def start(which):
        for has, copies in which:
            @pl.when(has)
            def _(copies=copies):
                copies.start()

    def arrive_edges(sent):
        arrive([(ways[j][3], sent[i][1]) for i, j in enumerate(opposite)])

    def arrive(which):
        for has, copies in which:
            @pl.when(has)
            def _(copies=copies):
                copies.wait_recv()

    lane = lax.broadcasted_iota(jnp.int32, (8, width), 1)
    group = lane // reach
    near_right = lane < width // 2

    def mask(m, rows):
        return jnp.broadcast_to(m[:1], (rows, width))

    def pack(tiles):
        rows = tiles[0].shape[0]
        turned = [t if k == 0 else pltpu.roll(t, reach * k, 1) for k, t in enumerate(tiles)]
        here, there = turned[0], turned[0]
        for k in range(1, planes):
            here = jnp.where(mask(group, rows) == k, turned[k], here)
            there = jnp.where(mask(group, rows) == k - 1, turned[k], there)
        return here.astype(BF), there.astype(BF)

    def unpack(edges, k):
        rows = edges.shape[0]
        tiles = (edges[:, :width], edges[:, width:])
        if k:
            tiles = [pltpu.roll(t, width - reach * k, 1) for t in tiles]
        return jnp.where(mask(near_right, rows), tiles[0], tiles[1]).astype(BF)

    local[0].wait()
    for p in range(planes):
        ext[middle, p * width:(p + 1) * width] = est_v[p].astype(BF)
    here, there = pack([est_v[p] for p in range(planes)])
    edge[0, middle], edge[1, middle] = here, there
    peers = 0
    for has, where in sides:
        peers = peers + has.astype(jnp.int32)
    pl.semaphore_wait(barrier, peers)
    start(((has_up, to_up[0]), (has_down, to_down[0])))
    start(est_ways)

    def clear(has, refs):
        @pl.when(jnp.logical_not(has))
        def _():
            for ref in refs:
                ref[...] = jnp.zeros(ref.shape, ref.dtype)

    clear(has_up, [ext.at[above]] + [quot.at[v, above] for v in range(views)])
    clear(has_down, [ext.at[below]] + [quot.at[v, below] for v in range(views)])
    for i, j in enumerate(opposite):
        s, _, dst, _, _ = ways[i]
        clear(ways[j][3], [side.at[s, dst]] + [qside.at[s, v, dst] for v in range(views)])

    taps = psf[...] / jnp.sum(psf[...], axis=1, keepdims=True)
    square = (width, width)
    apart = lax.broadcasted_iota(jnp.int32, square, 1) - lax.broadcasted_iota(jnp.int32, square, 0)
    near = (apart <= reach) & (apart >= -reach)
    for v in range(views):
        rows_y = jnp.broadcast_to(taps[v:v + 1], square)
        by = pltpu.roll(rows_y, 0, 1, stride=1, stride_axis=0)
        ky_s[v * height:(v + 1) * height, :] = by[:height, :inner].astype(BF)
        kt_s[v] = by.T[2 * reach:2 * reach + height, :inner].astype(BF)
        rows_x = jnp.broadcast_to(taps[views + v:views + v + 1], square)
        bx = pltpu.roll(rows_x, width - reach, 1, stride=1, stride_axis=0)
        core = jnp.where(near, bx, 0.0).astype(BF)
        off = jnp.where(near, 0.0, bx).astype(BF)
        df_s[v, :, :width] = core
        df_s[v, :, width:] = off
        da_s[v, :width, :] = core
        da_s[v, width:2 * width, :] = core
        da_s[v, 2 * width:, :] = off

    arrive(((has_up, to_down[0]), (has_down, to_up[0])))
    ybuf[...] = dot(ky_s[...], ext[...]).astype(BF)
    arrive_edges(est_ways)
    y_edges = dot(ky_s[...], jnp.concatenate([side[0], side[1]], axis=1))

    local[1].wait()
    for v in range(views):
        vs = slice(v * height, (v + 1) * height)
        parts = []
        for p in range(planes):
            halo = unpack(y_edges[vs], p)
            parts.append(jnp.concatenate([ybuf[vs, p * width:(p + 1) * width], halo], axis=1))
        blurred = dot(jnp.concatenate(parts, axis=0), df_s[v], 1)
        ratios = [
            views_v[v, p].astype(F32) / blurred[p * height:(p + 1) * height] for p in range(planes)
        ]
        for p in range(planes):
            quot[v, middle, p * width:(p + 1) * width] = ratios[p].astype(BF)
        if v % 2 == 0:
            start(((has_up, to_up[1 + v]), (has_down, to_down[1 + v])))
        qedge[0, v, middle], qedge[1, v, middle] = pack(ratios)
        if v % 2 == 1:
            start(quot_ways[v // 2])
            start(((has_up, to_up[1 + v]), (has_down, to_down[1 + v])))

    product = None
    for v in range(views):
        if v % 2 == 0:
            arrive_edges(quot_ways[v // 2])
        g_edges = dot(kt_s[v], jnp.concatenate([qside[0, v], qside[1, v]], axis=1))
        outer = dot(jnp.concatenate([unpack(g_edges, p) for p in range(planes)], axis=0), da_s[v, 2 * width:, :])
        arrive(((has_up, to_down[1 + v]), (has_down, to_up[1 + v])))
        g_own = dot(kt_s[v], quot[v])
        parts = []
        for p in range(planes):
            own = g_own[:, p * width:(p + 1) * width]
            high = own.astype(BF)
            parts.append(jnp.concatenate([high, (own - high.astype(F32)).astype(BF)], axis=1))
        corr = dot(jnp.concatenate(parts, axis=0), da_s[v, :2 * width, :]) + outer
        product = corr if product is None else product * corr
    out_ref[...] = est_v[...] * jnp.sqrt(jnp.sqrt(product)).reshape(planes, height, width)

    sent = [(has_up, to_up), (has_down, to_down)]
    sent += [(has, [copy]) for some in [est_ways] + quot_ways for has, copy in some]
    for has, copies in sent:
        @pl.when(has)
        def _(copies=copies):
            for copy in copies:
                copy.wait_send()


def local_step(nr, nc, estimate, views_data, psf_rows, psf_cols):
    views, planes, height, width = views_data.shape
    taps = psf_rows.shape[1]
    reach = (taps - 1) // 2
    inner = height + 2 * reach
    psf = jnp.concatenate([psf_rows, psf_cols])
    psf = jnp.pad(psf, ((0, 0), (0, width - taps)))
    vm = pltpu.VMEM
    any_spec = pl.BlockSpec(memory_space=pl.ANY)
    return pl.pallas_call(
        functools.partial(kernel, nr, nc, reach),
        out_shape=jax.ShapeDtypeStruct((planes, height, width), F32),
        in_specs=[any_spec] * 2 + [pl.BlockSpec(memory_space=pltpu.VMEM)],
        out_specs=pl.BlockSpec(memory_space=pltpu.VMEM),
        scratch_shapes=[
            vm((planes, height, width), F32),
            vm((views, planes, height, width), BF),
            vm((views * height, inner), BF),
            vm((views, height, inner), BF),
            vm((views, width, 2 * width), BF),
            vm((views, 3 * width, width), BF),
            vm((inner, planes * width), BF),
            vm((views * height, planes * width), BF),
            vm((views, inner, planes * width), BF),
            vm((2, inner, width), BF),
            vm((2, inner, width), BF),
            vm((2, views, inner, width), BF),
            vm((2, views, inner, width), BF),
            pltpu.SemaphoreType.DMA((2,)),
            pltpu.SemaphoreType.DMA((8 + 5 * views,)),
            pltpu.SemaphoreType.DMA((8 + 5 * views,)),
        ],
        compiler_params=pltpu.CompilerParams(
            collective_id=0, has_side_effects=True, vmem_limit_bytes=55036 * 1024
        ),
        name="deconvolve",
    )(estimate, views_data, psf)


def solution(mesh):
    nr, nc = mesh.shape["row"], mesh.shape["col"]
    return jax.shard_map(
        functools.partial(local_step, nr, nc),
        mesh=mesh,
        in_specs=(P(None, "row", "col"), P(None, None, "row", "col"), P(), P()),
        out_specs=P(None, "row", "col"),
        check_vma=False,
    )
```

```python
import functools

import jax
import jax.numpy as jnp
from jax import lax
from jax.experimental import pallas as pl
from jax.experimental.pallas import tpu as pltpu
from jax.sharding import PartitionSpec as P

BF = jnp.bfloat16
F32 = jnp.float32
MESH = pl.DeviceIdType.MESH


def dot(a, b, contract_b=0):
    return lax.dot_general(
        a, b, (((1,), (contract_b,)), ((), ())), preferred_element_type=F32
    )


def kernel(
    nr, nc, reach,
    est_hbm, views_hbm, psf, out_ref,
    est_v, views_v, ky_s, kt_s, df_s,
    ext, ybuf, quot, edge, side, qedge, qside,
    local_sem, send_sem, recv_sem,
):
    views, planes, height, width = views_v.shape
    inner = height + 2 * reach
    r, c = lax.axis_index("row"), lax.axis_index("col")
    up, down = (r - 1, c), (r + 1, c)
    left, right = (r, c - 1), (r, c + 1)
    has_up, has_down, has_left, has_right = r > 0, r < nr - 1, c > 0, c < nc - 1
    corners = (
        (has_up & has_left, (r - 1, c - 1)), (has_up & has_right, (r - 1, c + 1)),
        (has_down & has_left, (r + 1, c - 1)), (has_down & has_right, (r + 1, c + 1)),
    )
    sides = ((has_up, up), (has_down, down), (has_left, left), (has_right, right)) + corners

    local = [
        pltpu.make_async_copy(s, d, local_sem.at[i])
        for i, (s, d) in enumerate(((est_hbm, est_v), (views_hbm, views_v)))
    ]
    for copy in local:
        copy.start()

    barrier = pltpu.get_barrier_semaphore()
    for has, where in sides:
        @pl.when(has)
        def _():
            pl.semaphore_signal(barrier, inc=1, device_id=where, device_id_type=MESH)

    def remote(src, dst, slot, where):
        return pltpu.make_async_remote_copy(
            src_ref=src, dst_ref=dst, send_sem=send_sem.at[slot],
            recv_sem=recv_sem.at[slot], device_id=where, device_id_type=MESH,
        )

    first, last = pl.ds(reach, reach), pl.ds(height, reach)
    above, middle, below = pl.ds(0, reach), pl.ds(reach, height), pl.ds(reach + height, reach)
    quot_at, edge_at, pairs = 8, 8 + 2 * views, views // 2
    to_up = [remote(ext.at[first], ext.at[below], 0, up)] + [
        remote(quot.at[v, first], quot.at[v, below], quot_at + v, up) for v in range(views)
    ]
    to_down = [remote(ext.at[last], ext.at[above], 1, down)] + [
        remote(quot.at[v, last], quot.at[v, above], quot_at + views + v, down) for v in range(views)
    ]
    ways = (
        (0, middle, middle, has_left, left), (1, middle, middle, has_right, right),
        (0, first, below) + corners[0], (1, first, below) + corners[1],
        (0, last, above) + corners[2], (1, last, above) + corners[3],
    )
    opposite = (1, 0, 5, 4, 3, 2)
    est_ways = [
        (has, remote(edge.at[s, src], side.at[s, dst], 2 + i, where))
        for i, (s, src, dst, has, where) in enumerate(ways)
    ]
    quot_ways = [
        [
            (has, remote(
                qedge.at[s, pl.ds(2 * k, 2), src], qside.at[s, pl.ds(2 * k, 2), dst],
                edge_at + 6 * k + i, where,
            ))
            for i, (s, src, dst, has, where) in enumerate(ways)
        ]
        for k in range(pairs)
    ]

    def start(which):
        for has, copies in which:
            @pl.when(has)
            def _(copies=copies):
                copies.start()

    def arrive_edges(sent):
        arrive([(ways[j][3], sent[i][1]) for i, j in enumerate(opposite)])

    def arrive(which):
        for has, copies in which:
            @pl.when(has)
            def _(copies=copies):
                copies.wait_recv()

    lane = lax.broadcasted_iota(jnp.int32, (8, width), 1)
    group = lane // reach
    near_right = lane < width // 2

    def mask(m, rows):
        return jnp.broadcast_to(m[:1], (rows, width))

    def pack(tiles):
        rows = tiles[0].shape[0]
        turned = [t if k == 0 else pltpu.roll(t, reach * k, 1) for k, t in enumerate(tiles)]
        here, there = turned[0], turned[0]
        for k in range(1, planes):
            here = jnp.where(mask(group, rows) == k, turned[k], here)
            there = jnp.where(mask(group, rows) == k - 1, turned[k], there)
        return here.astype(BF), there.astype(BF)

    def unpack(edges, k):
        rows = edges.shape[0]
        tiles = (edges[:, :width], edges[:, width:])
        if k:
            tiles = [pltpu.roll(t, width - reach * k, 1) for t in tiles]
        return jnp.where(mask(near_right, rows), tiles[0], tiles[1]).astype(BF)

    local[0].wait()
    for p in range(planes):
        ext[middle, p * width:(p + 1) * width] = est_v[p].astype(BF)
    here, there = pack([est_v[p] for p in range(planes)])
    edge[0, middle], edge[1, middle] = here, there
    peers = 0
    for has, where in sides:
        peers = peers + has.astype(jnp.int32)
    pl.semaphore_wait(barrier, peers)
    start(((has_up, to_up[0]), (has_down, to_down[0])))
    start(est_ways)

    def clear(has, refs):
        @pl.when(jnp.logical_not(has))
        def _():
            for ref in refs:
                ref[...] = jnp.zeros(ref.shape, ref.dtype)

    clear(has_up, [ext.at[above]] + [quot.at[v, above] for v in range(views)])
    clear(has_down, [ext.at[below]] + [quot.at[v, below] for v in range(views)])
    for i, j in enumerate(opposite):
        s, _, dst, _, _ = ways[i]
        clear(ways[j][3], [side.at[s, dst]] + [qside.at[s, v, dst] for v in range(views)])

    taps = psf[...] / jnp.sum(psf[...], axis=1, keepdims=True)
    square = (width, width)
    apart = lax.broadcasted_iota(jnp.int32, square, 1) - lax.broadcasted_iota(jnp.int32, square, 0)
    near = (apart <= reach) & (apart >= -reach)
    for v in range(views):
        rows_y = jnp.broadcast_to(taps[v:v + 1], square)
        by = pltpu.roll(rows_y, 0, 1, stride=1, stride_axis=0)
        ky_s[v * height:(v + 1) * height, :] = by[:height, :inner].astype(BF)
        rows_x = jnp.broadcast_to(taps[views + v:views + v + 1], square)
        bx = pltpu.roll(rows_x, width - reach, 1, stride=1, stride_axis=0)
        core = jnp.where(near, bx, 0.0).astype(BF)
        off = jnp.where(near, 0.0, bx).astype(BF)
        df_s[v, :, :width] = core
        df_s[v, :, width:] = off

    arrive(((has_up, to_down[0]), (has_down, to_up[0])))
    ybuf[...] = dot(ky_s[...], ext[...]).astype(BF)
    arrive_edges(est_ways)
    y_edges = dot(ky_s[...], jnp.concatenate([side[0], side[1]], axis=1))

    local[1].wait()
    for v in range(views):
        vs = slice(v * height, (v + 1) * height)
        parts = []
        for p in range(planes):
            halo = unpack(y_edges[vs], p)
            parts.append(jnp.concatenate([ybuf[vs, p * width:(p + 1) * width], halo], axis=1))
        blurred = dot(jnp.concatenate(parts, axis=0), df_s[v], 1)
        ratios = [
            views_v[v, p].astype(F32) / blurred[p * height:(p + 1) * height] for p in range(planes)
        ]
        for p in range(planes):
            quot[v, middle, p * width:(p + 1) * width] = ratios[p].astype(BF)
        if v % 2 == 0:
            start(((has_up, to_up[1 + v]), (has_down, to_down[1 + v])))
        qedge[0, v, middle], qedge[1, v, middle] = pack(ratios)
        if v % 2 == 1:
            start(quot_ways[v // 2])
            start(((has_up, to_up[1 + v]), (has_down, to_down[1 + v])))

    for v in range(views):
        by = pltpu.roll(jnp.broadcast_to(taps[v:v + 1], square), 0, 1, stride=1, stride_axis=0)
        kt_s[v] = by.T[2 * reach:2 * reach + height, :inner].astype(BF)

    product = None
    for v in range(views):
        if v % 2 == 0:
            arrive_edges(quot_ways[v // 2])
        g_edges = dot(kt_s[v], jnp.concatenate([qside[0, v], qside[1, v]], axis=1))
        outer = dot(jnp.concatenate([unpack(g_edges, p) for p in range(planes)], axis=0), df_s[v, :, width:])
        arrive(((has_up, to_down[1 + v]), (has_down, to_up[1 + v])))
        g_own = dot(kt_s[v], quot[v])
        parts = []
        for p in range(planes):
            own = g_own[:, p * width:(p + 1) * width]
            high = own.astype(BF)
            parts.append(jnp.concatenate([high, (own - high.astype(F32)).astype(BF)], axis=1))
        corr = dot(
            jnp.concatenate(parts, axis=0), jnp.concatenate([df_s[v, :, :width]] * 2, axis=0)
        ) + outer
        product = corr if product is None else product * corr
    out_ref[...] = est_v[...] * jnp.sqrt(jnp.sqrt(product)).reshape(planes, height, width)

    sent = [(has_up, to_up), (has_down, to_down)]
    sent += [(has, [copy]) for some in [est_ways] + quot_ways for has, copy in some]
    for has, copies in sent:
        @pl.when(has)
        def _(copies=copies):
            for copy in copies:
                copy.wait_send()


def local_step(nr, nc, estimate, views_data, psf_rows, psf_cols):
    views, planes, height, width = views_data.shape
    taps = psf_rows.shape[1]
    reach = (taps - 1) // 2
    inner = height + 2 * reach
    psf = jnp.concatenate([psf_rows, psf_cols])
    psf = jnp.pad(psf, ((0, 0), (0, width - taps)))
    vm = pltpu.VMEM
    any_spec = pl.BlockSpec(memory_space=pl.ANY)
    return pl.pallas_call(
        functools.partial(kernel, nr, nc, reach),
        out_shape=jax.ShapeDtypeStruct((planes, height, width), F32),
        in_specs=[any_spec] * 2 + [pl.BlockSpec(memory_space=pltpu.VMEM)],
        out_specs=pl.BlockSpec(memory_space=pltpu.VMEM),
        scratch_shapes=[
            vm((planes, height, width), F32),
            vm((views, planes, height, width), BF),
            vm((views * height, inner), BF),
            vm((views, height, inner), BF),
            vm((views, width, 2 * width), BF),
            vm((inner, planes * width), BF),
            vm((views * height, planes * width), BF),
            vm((views, inner, planes * width), BF),
            vm((2, inner, width), BF),
            vm((2, inner, width), BF),
            vm((2, views, inner, width), BF),
            vm((2, views, inner, width), BF),
            pltpu.SemaphoreType.DMA((2,)),
            pltpu.SemaphoreType.DMA((8 + 5 * views,)),
            pltpu.SemaphoreType.DMA((8 + 5 * views,)),
        ],
        compiler_params=pltpu.CompilerParams(
            collective_id=0, has_side_effects=True, vmem_limit_bytes=55036 * 1024
        ),
        name="deconvolve",
    )(estimate, views_data, psf)


def solution(mesh):
    nr, nc = mesh.shape["row"], mesh.shape["col"]
    return jax.shard_map(
        functools.partial(local_step, nr, nc),
        mesh=mesh,
        in_specs=(P(None, "row", "col"), P(None, None, "row", "col"), P(), P()),
        out_specs=P(None, "row", "col"),
        check_vma=False,
    )
```

```python
import functools

import jax
import jax.numpy as jnp
from jax import lax
from jax.experimental import pallas as pl
from jax.experimental.pallas import tpu as pltpu
from jax.sharding import PartitionSpec as P

BF = jnp.bfloat16
F32 = jnp.float32
MESH = pl.DeviceIdType.MESH


def dot(a, b, contract_b=0):
    return lax.dot_general(
        a, b, (((1,), (contract_b,)), ((), ())), preferred_element_type=F32
    )


def kernel(
    nr, nc, reach,
    est_hbm, views_hbm, psf, out_ref,
    est_v, views_v, ky_s, kt_s, df_s,
    ext, ybuf, halo_s, quot, edge, side, qedge, qside,
    local_sem, send_sem, recv_sem,
):
    views, planes, height, width = views_v.shape
    inner = height + 2 * reach
    r, c = lax.axis_index("row"), lax.axis_index("col")
    up, down = (r - 1, c), (r + 1, c)
    left, right = (r, c - 1), (r, c + 1)
    has_up, has_down, has_left, has_right = r > 0, r < nr - 1, c > 0, c < nc - 1
    corners = (
        (has_up & has_left, (r - 1, c - 1)), (has_up & has_right, (r - 1, c + 1)),
        (has_down & has_left, (r + 1, c - 1)), (has_down & has_right, (r + 1, c + 1)),
    )
    sides = ((has_up, up), (has_down, down), (has_left, left), (has_right, right)) + corners

    local = [
        pltpu.make_async_copy(s, d, local_sem.at[i])
        for i, (s, d) in enumerate(((est_hbm, est_v), (views_hbm, views_v)))
    ]
    for copy in local:
        copy.start()

    barrier = pltpu.get_barrier_semaphore()
    for has, where in sides:
        @pl.when(has)
        def _():
            pl.semaphore_signal(barrier, inc=1, device_id=where, device_id_type=MESH)

    def remote(src, dst, slot, where):
        return pltpu.make_async_remote_copy(
            src_ref=src, dst_ref=dst, send_sem=send_sem.at[slot],
            recv_sem=recv_sem.at[slot], device_id=where, device_id_type=MESH,
        )

    first, last = pl.ds(reach, reach), pl.ds(height, reach)
    above, middle, below = pl.ds(0, reach), pl.ds(reach, height), pl.ds(reach + height, reach)
    quot_at, edge_at, pairs = 8, 8 + 2 * views, views // 2
    half = planes // 2

    def rows(v, which):
        return quot.at[v, which] if v else quot.at[v, which, pl.ds(half * width, half * width)]

    def early(which):
        return quot.at[0, which, pl.ds(0, half * width)]

    to_up = [remote(ext.at[first], ext.at[below], 0, up)] + [
        remote(rows(v, first), rows(v, below), quot_at + v, up) for v in range(views)
    ]
    to_up.append(remote(early(first), early(below), edge_at + 6 * pairs, up))
    to_down = [remote(ext.at[last], ext.at[above], 1, down)] + [
        remote(rows(v, last), rows(v, above), quot_at + views + v, down) for v in range(views)
    ]
    to_down.append(remote(early(last), early(above), edge_at + 6 * pairs + 1, down))
    ways = (
        (0, middle, middle, has_left, left), (1, middle, middle, has_right, right),
        (0, first, below) + corners[0], (1, first, below) + corners[1],
        (0, last, above) + corners[2], (1, last, above) + corners[3],
    )
    opposite = (1, 0, 5, 4, 3, 2)
    est_ways = [
        (has, remote(edge.at[s, src], side.at[s, dst], 2 + i, where))
        for i, (s, src, dst, has, where) in enumerate(ways)
    ]
    quot_ways = [
        [
            (has, remote(
                qedge.at[s, pl.ds(2 * k, 2), src], qside.at[s, pl.ds(2 * k, 2), dst],
                edge_at + 6 * k + i, where,
            ))
            for i, (s, src, dst, has, where) in enumerate(ways)
        ]
        for k in range(pairs)
    ]

    def start(which):
        for has, copies in which:
            @pl.when(has)
            def _(copies=copies):
                copies.start()

    def arrive_edges(sent):
        arrive([(ways[j][3], sent[i][1]) for i, j in enumerate(opposite)])

    def arrive(which):
        for has, copies in which:
            @pl.when(has)
            def _(copies=copies):
                copies.wait_recv()

    lane = lax.broadcasted_iota(jnp.int32, (8, width), 1)
    group = lane // reach
    near_right = lane < width // 2

    def mask(m, rows):
        return jnp.broadcast_to(m[:1], (rows, width))

    def pack(tiles):
        rows = tiles[0].shape[0]
        turned = [t if k == 0 else pltpu.roll(t, reach * k, 1) for k, t in enumerate(tiles)]
        here, there = turned[0], turned[0]
        for k in range(1, planes):
            here = jnp.where(mask(group, rows) == k, turned[k], here)
            there = jnp.where(mask(group, rows) == k - 1, turned[k], there)
        return here.astype(BF), there.astype(BF)

    def unpack(edges, k):
        rows = edges.shape[0]
        tiles = (edges[:, :width], edges[:, width:])
        if k:
            tiles = [pltpu.roll(t, width - reach * k, 1) for t in tiles]
        return jnp.where(mask(near_right, rows), tiles[0], tiles[1]).astype(BF)

    local[0].wait()
    for p in range(planes):
        ext[middle, p * width:(p + 1) * width] = est_v[p].astype(BF)
    here, there = pack([est_v[p] for p in range(planes)])
    edge[0, middle], edge[1, middle] = here, there
    peers = 0
    for has, where in sides:
        peers = peers + has.astype(jnp.int32)
    pl.semaphore_wait(barrier, peers)
    start(est_ways)
    start(((has_up, to_up[0]), (has_down, to_down[0])))

    def clear(has, refs):
        @pl.when(jnp.logical_not(has))
        def _():
            for ref in refs:
                ref[...] = jnp.zeros(ref.shape, ref.dtype)

    clear(has_up, [ext.at[above]] + [quot.at[v, above] for v in range(views)])
    clear(has_down, [ext.at[below]] + [quot.at[v, below] for v in range(views)])
    for i, j in enumerate(opposite):
        s, _, dst, _, _ = ways[i]
        clear(ways[j][3], [side.at[s, dst]] + [qside.at[s, v, dst] for v in range(views)])

    taps = psf[...] / jnp.sum(psf[...], axis=1, keepdims=True)
    square = (width, width)
    apart = lax.broadcasted_iota(jnp.int32, square, 1) - lax.broadcasted_iota(jnp.int32, square, 0)
    near = (apart <= reach) & (apart >= -reach)
    for v in range(views):
        rows_y = jnp.broadcast_to(taps[v:v + 1], square)
        by = pltpu.roll(rows_y, 0, 1, stride=1, stride_axis=0)
        ky_s[v * height:(v + 1) * height, :] = by[:height, :inner].astype(BF)
        rows_x = jnp.broadcast_to(taps[views + v:views + v + 1], square)
        bx = pltpu.roll(rows_x, width - reach, 1, stride=1, stride_axis=0)
        core = jnp.where(near, bx, 0.0).astype(BF)
        off = jnp.where(near, 0.0, bx).astype(BF)
        df_s[v, :, :width] = core
        df_s[v, :, width:] = off

    arrive_edges(est_ways)
    y_edges = dot(ky_s[...], jnp.concatenate([side[0], side[1]], axis=1))
    for v in range(views):
        for p in range(planes):
            halo_s[v, p] = unpack(y_edges[v * height:(v + 1) * height], p)
    arrive(((has_up, to_down[0]), (has_down, to_up[0])))
    ybuf[...] = dot(ky_s[...], ext[...]).astype(BF)

    local[1].wait()
    for v in range(views):
        vs = slice(v * height, (v + 1) * height)
        ratios = []
        for some in (range(half), range(half, planes)) if v == 0 else (range(planes),):
            parts = [
                jnp.concatenate([ybuf[vs, p * width:(p + 1) * width], halo_s[v, p]], axis=1)
                for p in some
            ]
            blurred = dot(jnp.concatenate(parts, axis=0), df_s[v], 1)
            for i, p in enumerate(some):
                ratios.append(views_v[v, p].astype(F32) / blurred[i * height:(i + 1) * height])
                quot[v, middle, p * width:(p + 1) * width] = ratios[p].astype(BF)
            if v == 0 and len(ratios) == half:
                start(((has_up, to_up[1 + views]), (has_down, to_down[1 + views])))
        if v % 2 == 0:
            start(((has_up, to_up[1 + v]), (has_down, to_down[1 + v])))
        qedge[0, v, middle], qedge[1, v, middle] = pack(ratios)
        if v % 2 == 1:
            start(quot_ways[v // 2])
            start(((has_up, to_up[1 + v]), (has_down, to_down[1 + v])))

    for v in range(views):
        by = pltpu.roll(jnp.broadcast_to(taps[v:v + 1], square), 0, 1, stride=1, stride_axis=0)
        kt_s[v] = by.T[2 * reach:2 * reach + height, :inner].astype(BF)

    product = None
    for v in range(views):
        if v % 2 == 0:
            arrive_edges(quot_ways[v // 2])
        g_edges = dot(kt_s[v], jnp.concatenate([qside[0, v], qside[1, v]], axis=1))
        outer = dot(jnp.concatenate([unpack(g_edges, p) for p in range(planes)], axis=0), df_s[v, :, width:])
        arrive(((has_up, to_down[1 + v]), (has_down, to_up[1 + v])))
        if v == 0:
            arrive(((has_up, to_down[1 + views]), (has_down, to_up[1 + views])))
        g_own = dot(kt_s[v], quot[v])
        parts = []
        for p in range(planes):
            own = g_own[:, p * width:(p + 1) * width]
            high = own.astype(BF)
            parts.append(jnp.concatenate([high, (own - high.astype(F32)).astype(BF)], axis=1))
        corr = dot(
            jnp.concatenate(parts, axis=0), jnp.concatenate([df_s[v, :, :width]] * 2, axis=0)
        ) + outer
        product = corr if product is None else product * corr
    out_ref[...] = est_v[...] * jnp.sqrt(jnp.sqrt(product)).reshape(planes, height, width)

    sent = [(has_up, to_up), (has_down, to_down)]
    sent += [(has, [copy]) for some in [est_ways] + quot_ways for has, copy in some]
    for has, copies in sent:
        @pl.when(has)
        def _(copies=copies):
            for copy in copies:
                copy.wait_send()


def local_step(nr, nc, estimate, views_data, psf_rows, psf_cols):
    views, planes, height, width = views_data.shape
    taps = psf_rows.shape[1]
    reach = (taps - 1) // 2
    inner = height + 2 * reach
    psf = jnp.concatenate([psf_rows, psf_cols])
    psf = jnp.pad(psf, ((0, 0), (0, width - taps)))
    vm = pltpu.VMEM
    any_spec = pl.BlockSpec(memory_space=pl.ANY)
    return pl.pallas_call(
        functools.partial(kernel, nr, nc, reach),
        out_shape=jax.ShapeDtypeStruct((planes, height, width), F32),
        in_specs=[any_spec] * 2 + [pl.BlockSpec(memory_space=pltpu.VMEM)],
        out_specs=pl.BlockSpec(memory_space=pltpu.VMEM),
        scratch_shapes=[
            vm((planes, height, width), F32),
            vm((views, planes, height, width), BF),
            vm((views * height, inner), BF),
            vm((views, height, inner), BF),
            vm((views, width, 2 * width), BF),
            vm((inner, planes * width), BF),
            vm((views * height, planes * width), BF),
            vm((views, planes, height, width), BF),
            vm((views, inner, planes * width), BF),
            vm((2, inner, width), BF),
            vm((2, inner, width), BF),
            vm((2, views, inner, width), BF),
            vm((2, views, inner, width), BF),
            pltpu.SemaphoreType.DMA((2,)),
            pltpu.SemaphoreType.DMA((10 + 5 * views,)),
            pltpu.SemaphoreType.DMA((10 + 5 * views,)),
        ],
        compiler_params=pltpu.CompilerParams(
            collective_id=0, has_side_effects=True, vmem_limit_bytes=55036 * 1024
        ),
        name="deconvolve",
    )(estimate, views_data, psf)


def solution(mesh):
    nr, nc = mesh.shape["row"], mesh.shape["col"]
    return jax.shard_map(
        functools.partial(local_step, nr, nc),
        mesh=mesh,
        in_specs=(P(None, "row", "col"), P(None, None, "row", "col"), P(), P()),
        out_specs=P(None, "row", "col"),
        check_vma=False,
    )
```

```python
import functools

import jax
import jax.numpy as jnp
from jax import lax
from jax.experimental import pallas as pl
from jax.experimental.pallas import tpu as pltpu
from jax.sharding import PartitionSpec as P

BF = jnp.bfloat16
F32 = jnp.float32
MESH = pl.DeviceIdType.MESH


def dot(a, b, contract_b=0):
    return lax.dot_general(
        a, b, (((1,), (contract_b,)), ((), ())), preferred_element_type=F32
    )


def kernel(
    nr, nc, reach,
    est_hbm, views_hbm, psf, out_ref,
    est_v, views_v, ky_s, kt_s, df_s, da_s,
    ext, ybuf, quot, edge, side, qedge, qside,
    local_sem, send_sem, recv_sem,
):
    views, planes, height, width = views_v.shape
    inner = height + 2 * reach
    r, c = lax.axis_index("row"), lax.axis_index("col")
    up, down = (r - 1, c), (r + 1, c)
    left, right = (r, c - 1), (r, c + 1)
    has_up, has_down, has_left, has_right = r > 0, r < nr - 1, c > 0, c < nc - 1
    corners = (
        (has_up & has_left, (r - 1, c - 1)), (has_up & has_right, (r - 1, c + 1)),
        (has_down & has_left, (r + 1, c - 1)), (has_down & has_right, (r + 1, c + 1)),
    )
    sides = ((has_up, up), (has_down, down), (has_left, left), (has_right, right)) + corners

    local = [
        pltpu.make_async_copy(s, d, local_sem.at[i])
        for i, (s, d) in enumerate(((est_hbm, est_v), (views_hbm, views_v)))
    ]
    for copy in local:
        copy.start()

    barrier = pltpu.get_barrier_semaphore()
    for has, where in sides:
        @pl.when(has)
        def _():
            pl.semaphore_signal(barrier, inc=1, device_id=where, device_id_type=MESH)

    def remote(src, dst, slot, where):
        return pltpu.make_async_remote_copy(
            src_ref=src, dst_ref=dst, send_sem=send_sem.at[slot],
            recv_sem=recv_sem.at[slot], device_id=where, device_id_type=MESH,
        )

    first, last = pl.ds(reach, reach), pl.ds(height, reach)
    above, middle, below = pl.ds(0, reach), pl.ds(reach, height), pl.ds(reach + height, reach)
    quot_at, edge_at, pairs = 8, 8 + 2 * views, views // 2
    to_up = [remote(ext.at[first], ext.at[below], 0, up)] + [
        remote(quot.at[v, first], quot.at[v, below], quot_at + v, up) for v in range(views)
    ]
    to_down = [remote(ext.at[last], ext.at[above], 1, down)] + [
        remote(quot.at[v, last], quot.at[v, above], quot_at + views + v, down) for v in range(views)
    ]
    ways = (
        (0, middle, middle, has_left, left), (1, middle, middle, has_right, right),
        (0, first, below) + corners[0], (1, first, below) + corners[1],
        (0, last, above) + corners[2], (1, last, above) + corners[3],
    )
    opposite = (1, 0, 5, 4, 3, 2)
    est_ways = [
        (has, remote(edge.at[s, src], side.at[s, dst], 2 + i, where))
        for i, (s, src, dst, has, where) in enumerate(ways)
    ]
    quot_ways = [
        [
            (has, remote(
                qedge.at[s, pl.ds(2 * k, 2), src], qside.at[s, pl.ds(2 * k, 2), dst],
                edge_at + 6 * k + i, where,
            ))
            for i, (s, src, dst, has, where) in enumerate(ways)
        ]
        for k in range(pairs)
    ]

    def start(which):
        for has, copies in which:
            @pl.when(has)
            def _(copies=copies):
                copies.start()

    def arrive_edges(sent):
        arrive([(ways[j][3], sent[i][1]) for i, j in enumerate(opposite)])

    def arrive(which):
        for has, copies in which:
            @pl.when(has)
            def _(copies=copies):
                copies.wait_recv()

    lane = lax.broadcasted_iota(jnp.int32, (8, width), 1)
    group = lane // reach
    near_right = lane < width // 2

    def mask(m, rows):
        return jnp.broadcast_to(m[:1], (rows, width))

    def pack(tiles):
        rows = tiles[0].shape[0]
        turned = [t if k == 0 else pltpu.roll(t, reach * k, 1) for k, t in enumerate(tiles)]
        here, there = turned[0], turned[0]
        for k in range(1, planes):
            here = jnp.where(mask(group, rows) == k, turned[k], here)
            there = jnp.where(mask(group, rows) == k - 1, turned[k], there)
        return here.astype(BF), there.astype(BF)

    def unpack(edges, k):
        rows = edges.shape[0]
        tiles = (edges[:, :width], edges[:, width:])
        if k:
            tiles = [pltpu.roll(t, width - reach * k, 1) for t in tiles]
        return jnp.where(mask(near_right, rows), tiles[0], tiles[1]).astype(BF)

    local[0].wait()
    for p in range(planes):
        ext[middle, p * width:(p + 1) * width] = est_v[p].astype(BF)
    here, there = pack([est_v[p] for p in range(planes)])
    edge[0, middle], edge[1, middle] = here, there
    peers = 0
    for has, where in sides:
        peers = peers + has.astype(jnp.int32)
    pl.semaphore_wait(barrier, peers)
    start(((has_up, to_up[0]), (has_down, to_down[0])))
    start(est_ways)

    def clear(has, refs):
        @pl.when(jnp.logical_not(has))
        def _():
            for ref in refs:
                ref[...] = jnp.zeros(ref.shape, ref.dtype)

    clear(has_up, [ext.at[above]] + [quot.at[v, above] for v in range(views)])
    clear(has_down, [ext.at[below]] + [quot.at[v, below] for v in range(views)])
    for i, j in enumerate(opposite):
        s, _, dst, _, _ = ways[i]
        clear(ways[j][3], [side.at[s, dst]] + [qside.at[s, v, dst] for v in range(views)])

    taps = psf[...] / jnp.sum(psf[...], axis=1, keepdims=True)
    square = (width, width)
    apart = lax.broadcasted_iota(jnp.int32, square, 1) - lax.broadcasted_iota(jnp.int32, square, 0)
    near = (apart <= reach) & (apart >= -reach)
    for v in range(views):
        rows_y = jnp.broadcast_to(taps[v:v + 1], square)
        by = pltpu.roll(rows_y, 0, 1, stride=1, stride_axis=0)
        ky_s[v * height:(v + 1) * height, :] = by[:height, :inner].astype(BF)
        kt_s[v] = by.T[2 * reach:2 * reach + height, :inner].astype(BF)
        rows_x = jnp.broadcast_to(taps[views + v:views + v + 1], square)
        bx = pltpu.roll(rows_x, width - reach, 1, stride=1, stride_axis=0)
        core = jnp.where(near, bx, 0.0).astype(BF)
        off = jnp.where(near, 0.0, bx).astype(BF)
        df_s[v, :, :width] = core
        df_s[v, :, width:] = off
        da_s[v, :width, :] = core
        da_s[v, width:, :] = off

    arrive(((has_up, to_down[0]), (has_down, to_up[0])))
    ybuf[...] = dot(ky_s[...], ext[...]).astype(BF)
    arrive_edges(est_ways)
    y_edges = dot(ky_s[...], jnp.concatenate([side[0], side[1]], axis=1))

    local[1].wait()
    for v in range(views):
        vs = slice(v * height, (v + 1) * height)
        parts = []
        for p in range(planes):
            halo = unpack(y_edges[vs], p)
            parts.append(jnp.concatenate([ybuf[vs, p * width:(p + 1) * width], halo], axis=1))
        blurred = dot(jnp.concatenate(parts, axis=0), df_s[v], 1)
        ratios = [
            views_v[v, p].astype(F32) / blurred[p * height:(p + 1) * height] for p in range(planes)
        ]
        for p in range(planes):
            quot[v, middle, p * width:(p + 1) * width] = ratios[p].astype(BF)
        if v < views - 1:
            start(((has_up, to_up[1 + v]), (has_down, to_down[1 + v])))
        qedge[0, v, middle], qedge[1, v, middle] = pack(ratios)
        if v % 2 == 1:
            start(quot_ways[v // 2])
        if v == views - 1:
            start(((has_up, to_up[1 + v]), (has_down, to_down[1 + v])))

    product = None
    for v in range(views):
        arrive(((has_up, to_down[1 + v]), (has_down, to_up[1 + v])))
        g_own = dot(kt_s[v], quot[v])
        if v % 2 == 0:
            arrive_edges(quot_ways[v // 2])
        g_edges = dot(kt_s[v], jnp.concatenate([qside[0, v], qside[1, v]], axis=1))
        parts, rest = [], []
        for p in range(planes):
            own = g_own[:, p * width:(p + 1) * width]
            high = own.astype(BF)
            rest.append((own - high.astype(F32)).astype(BF))
            parts.append(jnp.concatenate([high, unpack(g_edges, p)], axis=1))
        corr = dot(jnp.concatenate(parts, axis=0), da_s[v])
        corr = corr + dot(jnp.concatenate(rest, axis=0), da_s[v, :width, :])
        product = corr if product is None else product * corr
    out_ref[...] = est_v[...] * jnp.sqrt(jnp.sqrt(product)).reshape(planes, height, width)

    sent = [(has_up, to_up), (has_down, to_down)]
    sent += [(has, [copy]) for some in [est_ways] + quot_ways for has, copy in some]
    for has, copies in sent:
        @pl.when(has)
        def _(copies=copies):
            for copy in copies:
                copy.wait_send()


def local_step(nr, nc, estimate, views_data, psf_rows, psf_cols):
    views, planes, height, width = views_data.shape
    taps = psf_rows.shape[1]
    reach = (taps - 1) // 2
    inner = height + 2 * reach
    psf = jnp.concatenate([psf_rows, psf_cols])
    psf = jnp.pad(psf, ((0, 0), (0, width - taps)))
    vm = pltpu.VMEM
    any_spec = pl.BlockSpec(memory_space=pl.ANY)
    return pl.pallas_call(
        functools.partial(kernel, nr, nc, reach),
        out_shape=jax.ShapeDtypeStruct((planes, height, width), F32),
        in_specs=[any_spec] * 2 + [pl.BlockSpec(memory_space=pltpu.VMEM)],
        out_specs=pl.BlockSpec(memory_space=pltpu.VMEM),
        scratch_shapes=[
            vm((planes, height, width), F32),
            vm((views, planes, height, width), BF),
            vm((views * height, inner), BF),
            vm((views, height, inner), BF),
            vm((views, width, 2 * width), BF),
            vm((views, 2 * width, width), BF),
            vm((inner, planes * width), BF),
            vm((views * height, planes * width), BF),
            vm((views, inner, planes * width), BF),
            vm((2, inner, width), BF),
            vm((2, inner, width), BF),
            vm((2, views, inner, width), BF),
            vm((2, views, inner, width), BF),
            pltpu.SemaphoreType.DMA((2,)),
            pltpu.SemaphoreType.DMA((8 + 5 * views,)),
            pltpu.SemaphoreType.DMA((8 + 5 * views,)),
        ],
        compiler_params=pltpu.CompilerParams(
            collective_id=0, has_side_effects=True, vmem_limit_bytes=55036 * 1024
        ),
        name="deconvolve",
    )(estimate, views_data, psf)


def solution(mesh):
    nr, nc = mesh.shape["row"], mesh.shape["col"]
    return jax.shard_map(
        functools.partial(local_step, nr, nc),
        mesh=mesh,
        in_specs=(P(None, "row", "col"), P(None, None, "row", "col"), P(), P()),
        out_specs=P(None, "row", "col"),
        check_vma=False,
    )
```
